256 devices in a mesh: rep: 2 (over core), expert: 128 (over z, y, x).
Axes of the slice: x: 4, y: 4, z: 8, core: 2. Of those that a mesh axis runs over, the one named last changes fastest.
Arguments:
- tokens: bfloat16 [32768, 1024], P(('rep', 'expert')), may hold values from -6 to 6
- cotangent: bfloat16 [32768, 1024], P(('rep', 'expert')), may hold values from -6 to 6
- gate_values: float32 [32768, 2], P(('rep', 'expert')), may hold values from 0.2 to 1
- expert_ids: int32 [32768, 2], P(('rep', 'expert')), may hold values from 0 to 127, all different within a row; in each aligned block of 128 rows (0 to 127, 128 to 255, ...) at most 4 rows name the same one
- keep_second: int32 [32768], P(('rep', 'expert')), may hold values 0 or 1
- weight_in: bfloat16 [128, 1024, 1024], P('expert'), may hold values from -0.1875 to 0.1875
- weight_out: bfloat16 [128, 1024, 1024], P('expert'), may hold values from -0.1875 to 0.1875
Outputs:
- grad_tokens: bfloat16 [32768, 1024], P(('rep', 'expert'))
- grad_gates: float32 [32768, 2], P(('rep', 'expert'))
- grad_weight_in: bfloat16 [128, 1024, 1024], P('expert', None, 'rep')
- grad_weight_out: bfloat16 [128, 1024, 1024], P('expert', None, 'rep')
The draws below stay inside these ranges and needn't reach their ends.
Inputs may be any that keep to these rules, and one draw needn't show every extreme that they name: `expert_ids`: in each group of 128 tokens no expert is named by more than 4 tokens, a bound that some block reaches; a token's two experts differ.
All inputs are finite; a program needn't handle non-finite values. No bound on the sum of `keep_second` on one device may be relied on, other than what follows from the above.
Results may differ from the reference program's by a relative error of at most 0.022.
Values may be sent and summed in bfloat16 or wider, within the bound.
A program may use at most 128 MiB of HBM per device.

```python
import math
import jax
import jax.numpy as jnp
import numpy as np
from jax import lax

D = 1024
F = 1024
TOK_DEV = 128
CAP = 4
EXPERTS = 128
TOKENS = 32768
N_REP = 2
N_EXPERT = 128


def plant(values, stream_key, least, largest):
    longest = values.shape.index(max(values.shape))
    spots = []
    for shift in (0, 1):
        where = [jax.random.randint(jax.random.fold_in(stream_key, axis), (), 0, length) for axis, length in enumerate(values.shape)]
        where[longest] = (where[longest] + shift) % values.shape[longest]
        spots.append(tuple(where))
    return values.at[spots[0]].set(least).at[spots[1]].set(largest)


def shard_levels(rng, dims, split, smallest, high):
    loudness, own = 1.0, jax.random.fold_in(rng, 6)
    for dim, shards_of in split:
        heights = jnp.exp(jax.random.uniform(jax.random.fold_in(own, dim), (shards_of,), jnp.float32, smallest / len(split), high / len(split)))
        loudness = loudness * jnp.repeat(heights, dims[dim] // shards_of).reshape([-1 if axis == dim else 1 for axis in range(len(dims))])
    return loudness


def shared_out(own_key, own, number, rows, count, top, most, lean):
    sequence = jax.random.permutation(own_key, count)
    heavy_load, ordinary = load_shares(count, rows * top, most, lean, True), load_shares(count, rows * top, most, lean, False)
    places = jnp.arange(count)

    def named(tallies, rotation):
        used = int((tallies > 0).sum())
        fixed = max(1, used // 4)
        passed = fixed + (places - fixed + rotation * (used - fixed)) % max(1, count - fixed)
        return jnp.zeros((count,), jnp.int32).at[sequence[jnp.where(places < fixed, places, passed)]].set(jnp.asarray(tallies, jnp.int32))

    tallies = jnp.where(number % 4 == 0, named(heavy_load, number // 4), named(ordinary, number - number // 4 - 1))
    mixed = jax.random.permutation(jax.random.fold_in(own, 3), count)
    giver, taker = mixed[0:count // 2 * 2:2], mixed[1:count // 2 * 2:2]
    margin = jnp.minimum(tallies[giver] - 1, most - tallies[taker]) // 2
    margin = jnp.where((giver == sequence[0]) | (taker == sequence[0]) | (tallies[taker] == 0), 0, jnp.maximum(margin, 0))
    passed = jax.random.randint(jax.random.fold_in(own, 4), (count // 2,), 0, 1 << 20) % (margin + 1)
    tallies = tallies.at[giver].add(-passed).at[taker].add(passed)
    labels = jnp.searchsorted(jnp.cumsum(tallies), jnp.arange(rows * top), side="right").astype(jnp.int32)
    grid = labels.reshape(top, rows).T
    grid = grid[jax.random.permutation(jax.random.fold_in(own, 1), rows)]
    rotation = jax.random.randint(jax.random.fold_in(own, 2), (rows, 1), 0, top)
    return jnp.take_along_axis(grid, (jnp.arange(top)[None, :] + rotation) % top, axis=1)


def load_shares(count, total, reach, skew, full):
    loads = [(1 << 20) // math.isqrt(grade ** skew) + 1 for grade in range(1, count + 1)]
    largest = reach if full else min(reach, max(-(-total // count), total * loads[0] // sum(loads)))
    least = 1 if total - largest >= count - 1 else 0
    counts, rest = [largest] + [least] * (count - 1), total - largest - least * (count - 1)
    while rest > 0:
        candidates = [i for i in range(1, count) if counts[i] < largest] or [i for i in range(1, count) if counts[i] < reach]
        pool, remaining = sum([loads[i] for i in candidates]), rest
        for i in candidates:
            extra = min(reach - counts[i], max(1, remaining * loads[i] // pool), rest)
            counts[i] = counts[i] + extra
            rest = rest - extra
    return np.array(counts)


def noise(own_key, dims, spread, reach, split=(), held_as=jnp.bfloat16):
    entries = spread * jax.random.normal(own_key, dims, jnp.float32)
    if split:
        entries = entries * shard_levels(own_key, dims, split, -0.22, 0.18)
    return jnp.clip(entries, -reach, reach).astype(held_as)


def setup_inputs(seed: int = 0) -> dict:
    keys = jax.random.split(jax.random.key(seed), 8)
    tokens = noise(keys[0], (TOKENS, D), 1.0, 6.0, ((0, 256),))
    cotangent = noise(keys[1], (TOKENS, D), 1.0, 6.0, ((0, 256),))
    gate_values = jnp.clip(0.2 + 0.8 * jax.random.uniform(keys[2], (TOKENS, 2), jnp.float32) ** shard_levels(keys[2], (TOKENS, 2), ((0, 256),), -0.2, 0.2), 0.2, 1.0)
    expert_ids_keys = jax.random.split(jax.random.fold_in(keys[3], 1), TOKENS // TOK_DEV)
    expert_ids_turns = jax.random.permutation(jax.random.fold_in(keys[3], 3), TOKENS // TOK_DEV)
    expert_ids = jax.vmap(lambda own, number: shared_out(jax.random.fold_in(keys[3], 2), own, number, TOK_DEV, EXPERTS, 2, CAP, 2))(expert_ids_keys, expert_ids_turns).reshape((TOKENS, 2))
    keep_second = plant((jax.random.randint(keys[4], (TOKENS,), 0, 4) < 3).astype(jnp.int32), jax.random.fold_in(keys[4], 1), 0, 1)
    weight_in = noise(keys[5], (EXPERTS, D, F), D ** -0.5, 0.1875, ((0, 128),))
    weight_out = noise(keys[6], (EXPERTS, F, D), F ** -0.5, 0.1875, ((0, 128),))
    return {"tokens": tokens, "cotangent": cotangent, "gate_values": gate_values, "expert_ids": expert_ids, "keep_second": keep_second, "weight_in": weight_in, "weight_out": weight_out}


def gelu_value(pre):
    const = 0.7978845608028654
    inner = jnp.tanh(const * (pre + 0.044715 * pre * pre * pre))
    return 0.5 * pre * (1.0 + inner)


def gelu_slope(pre):
    const = 0.7978845608028654
    inner = jnp.tanh(const * (pre + 0.044715 * pre * pre * pre))
    return 0.5 * (1.0 + inner) + 0.5 * pre * (1.0 - inner * inner) * const * (1.0 + 3.0 * 0.044715 * pre * pre)


def expert_work(x_rows, cot_rows, scale_rows, proj_in, proj_out):
    pre = jnp.dot(x_rows, proj_in, preferred_element_type=jnp.float32)
    act = gelu_value(pre).astype(jnp.bfloat16)
    outval = jnp.dot(act, proj_out, preferred_element_type=jnp.float32)
    score = jnp.sum(cot_rows.astype(jnp.float32) * outval, axis=1)
    grad_output = (scale_rows[:, None] * cot_rows.astype(jnp.float32)).astype(jnp.bfloat16)
    grad_act = jnp.dot(grad_output, proj_out.T, preferred_element_type=jnp.float32)
    grad_pre = (grad_act * gelu_slope(pre)).astype(jnp.bfloat16)
    grad_assign = jnp.dot(grad_pre, proj_in.T, preferred_element_type=jnp.float32).astype(jnp.bfloat16)
    grad_out_w = jnp.dot(act.T, grad_output, preferred_element_type=jnp.float32)
    grad_in_w = jnp.dot(x_rows.T, grad_pre, preferred_element_type=jnp.float32)
    return grad_assign, score, grad_in_w, grad_out_w


def reference(tokens, cotangent, gate_values, expert_ids, keep_second, weight_in, weight_out):
    groups = N_REP * N_EXPERT
    width = tokens.shape[1]
    ids = expert_ids.reshape(groups, TOK_DEV, 2)
    assign_exp = jnp.concatenate([ids[:, :, 0], ids[:, :, 1]], axis=1)
    onehot = (assign_exp[:, :, None] == jnp.arange(EXPERTS, dtype=jnp.int32)[None, None, :]).astype(jnp.int32)
    before = jnp.cumsum(onehot, axis=1) - onehot
    position = jnp.sum(before * onehot, axis=2).astype(jnp.int32)
    group_idx = jnp.arange(groups, dtype=jnp.int32)[:, None]
    slot = group_idx * CAP + position
    total = groups * 2 * TOK_DEV
    global_idx = jnp.arange(total, dtype=jnp.int32).reshape(groups, 2 * TOK_DEV)
    table = jnp.full((EXPERTS, groups * CAP), total, jnp.int32).at[assign_exp, slot].set(global_idx)
    token_of = group_idx * TOK_DEV + (jnp.arange(2 * TOK_DEV, dtype=jnp.int32) % TOK_DEV)[None, :]
    token_table = jnp.concatenate([token_of.reshape(-1), jnp.full((1,), TOKENS, jnp.int32)])
    gate_grp = gate_values.reshape(groups, TOK_DEV, 2)
    keep_grp = keep_second.reshape(groups, TOK_DEV).astype(jnp.float32)
    scale = jnp.concatenate([gate_grp[:, :, 0], gate_grp[:, :, 1] * keep_grp], axis=1)
    scale_table = jnp.concatenate([scale.reshape(-1), jnp.zeros((1,), jnp.float32)])
    x_padded = jnp.concatenate([tokens, jnp.zeros((1, width), tokens.dtype)], axis=0)
    cot_padded = jnp.concatenate([cotangent, jnp.zeros((1, width), cotangent.dtype)], axis=0)

    def per_expert(packed):
        rows, proj_in, proj_out = packed
        token_rows = token_table[rows]
        grad_assign, score, grad_in_w, grad_out_w = expert_work(
            x_padded[token_rows], cot_padded[token_rows], scale_table[rows], proj_in, proj_out)
        return grad_assign, score, grad_in_w.astype(jnp.bfloat16), grad_out_w.astype(jnp.bfloat16)

    grad_assign, score, grad_weight_in, grad_weight_out = lax.map(per_expert, (table, weight_in, weight_out))
    flat_rows = table.reshape(-1)
    assign_grad = jnp.zeros((total + 1, width), jnp.float32).at[flat_rows].set(
        grad_assign.reshape(-1, width).astype(jnp.float32))
    assign_score = jnp.zeros((total + 1,), jnp.float32).at[flat_rows].set(score.reshape(-1))
    per_token = assign_grad[:total].reshape(groups, 2, TOK_DEV, width)
    grad_tokens = (per_token[:, 0] + per_token[:, 1]).reshape(TOKENS, width).astype(jnp.bfloat16)
    score_grp = assign_score[:total].reshape(groups, 2, TOK_DEV)
    grad_gates = jnp.stack([score_grp[:, 0], score_grp[:, 1] * keep_grp], axis=2).reshape(TOKENS, 2)
    return grad_tokens, grad_gates, grad_weight_in, grad_weight_out
```

```python
import functools

import jax
import jax.numpy as jnp
from jax import lax
from jax.experimental import pallas as pl
from jax.experimental.pallas import tpu as pltpu
from jax.sharding import PartitionSpec as P

MESH = pl.DeviceIdType.MESH
F32, BF16, I32 = jnp.float32, jnp.bfloat16, jnp.int32
NZ, NY, NX = 8, 4, 4
PLANE = NY * NX
EXPERTS = NZ * PLANE
CAP = 4
TOK = 128
D = 1024
F = 1024
HALF = 512
ORDER = (3, 5, 4, 0, 2, 6, 1, 7)
CHUNKS = 4
BLOCKS = EXPERTS // CHUNKS
ROWS = BLOCKS * 16
SLOTS = BLOCKS * CAP
SELF_CHUNK, SELF_BLOCK = ORDER.index(0) // 2, (ORDER.index(0) % 2) * PLANE


def dot(a, b, contract):
    return lax.dot_general(a, b, (contract, ((), ())), preferred_element_type=F32)


def iota(shape, dim):
    return lax.broadcasted_iota(I32, shape, dim)


def gelu_parts(pre):
    const = 0.7978845608028654
    square = pre * pre
    inner = jnp.tanh(const * (pre + 0.044715 * square * pre))
    half = 0.5 * (1.0 + inner)
    slope = half + 0.5 * pre * (1.0 - inner * inner) * (
        const * (1.0 + 3.0 * 0.044715 * square)
    )
    return pre * half, slope


def kernel(
    tokens_ref, cot_ref, gates_ref, ids_ref, keep_ref, win_hbm, wout_hbm,
    gtok_ref, ggate_ref, gwin_ref, gwout_ref,
    win, wout, xcat, send, recv, ret, back, score_ret, score_back,
    xrows, gorows, actrows, gprows, perm, wg_send, wg_recv, colcode, total,
    load_sem, self_sem, send_sem, recv_sem, ret_sem, back_sem,
    sret_sem, sback_sem, wgs_sem, wgr_sem,
):
    me = lax.axis_index("expert")
    rep = lax.axis_index("rep")
    my_z, my_y, my_x = me // PLANE, (me // NX) % NY, me % NX

    bar = pltpu.get_barrier_semaphore()

    def greet(i, carry):
        pl.semaphore_signal(bar, inc=1, device_id=(rep, (me + i) % EXPERTS), device_id_type=MESH)
        return carry

    lax.fori_loop(1, EXPERTS, greet, 0)
    pl.semaphore_signal(bar, inc=1, device_id=(1 - rep, me), device_id_type=MESH)

    load_in = pltpu.make_async_copy(win_hbm.at[0], win, load_sem.at[0])
    load_out = pltpu.make_async_copy(wout_hbm.at[0], wout, load_sem.at[1])
    load_in.start()
    load_out.start()

    ids = ids_ref[...]
    dz = (ids // PLANE - my_z + NZ) % NZ
    dy = ((ids // NX) % NY - my_y + NY) % NY
    dx = (ids % NX - my_x + NX) % NX
    pz = jnp.zeros_like(dz)
    for at, off in enumerate(ORDER):
        pz = jnp.where(dz == off, at, pz)
    place = pz * PLANE + dy * NX + dx
    first, second = place[0:1], place[1:2]
    hot0 = jnp.where(iota((EXPERTS, TOK), 0) == first, 1.0, 0.0)
    hot1 = jnp.where(iota((EXPERTS, TOK), 0) == second, 1.0, 0.0)
    upper = jnp.where(iota((TOK, TOK), 0) < iota((TOK, TOK), 1), 1.0, 0.0).astype(BF16)
    plain = ((1,), (0,))
    before0 = dot(hot0.astype(BF16), upper, plain)
    before1 = dot(hot1.astype(BF16), upper, plain) + jnp.sum(hot0, axis=1, keepdims=True)
    pos0 = jnp.sum(hot0 * before0, axis=0, keepdims=True)
    pos1 = jnp.sum(hot1 * before1, axis=0, keepdims=True)
    code0 = first * 16 + pos0.astype(I32)
    code1 = second * 16 + pos1.astype(I32)
    gate_low = gates_ref[...].astype(BF16).astype(F32)
    scale0 = gate_low[0:1]
    scale1 = gate_low[1:2] * keep_ref[...].astype(F32)
    one = jnp.ones_like(scale0)
    quad0 = jnp.concatenate([code0 + 4 * q for q in range(4)], axis=1)
    quad1 = jnp.concatenate([code1 + 4 * q for q in range(4)], axis=1)
    weight0 = jnp.concatenate([one, one, scale0, scale0], axis=1)
    weight1 = jnp.concatenate([one, one, scale1, scale1], axis=1)

    xcat[0:128, :] = tokens_ref[:, 0:HALF]
    xcat[128:256, :] = tokens_ref[:, HALF:]
    xcat[256:384, :] = cot_ref[:, 0:HALF]
    xcat[384:512, :] = cot_ref[:, HALF:]

    def target(c, b, sign):
        lead = b // PLANE
        off = ORDER[2 * c] + (ORDER[2 * c + 1] - ORDER[2 * c]) * lead
        return (
            rep,
            ((my_z + sign * off + NZ) % NZ) * PLANE
            + ((my_y + sign * ((b // NX) % NY) + NY) % NY) * NX
            + (my_x + sign * (b % NX) + NX) % NX,
        )

    def gather(c):
        row = iota((ROWS, 512), 0) + c * ROWS
        pick = jnp.where(row == quad0, weight0, jnp.where(row == quad1, weight1, 0.0))
        block = dot(pick.astype(BF16), xcat[...], plain).astype(BF16)
        send[c] = block.reshape(BLOCKS, 16, HALF)

    def spans(c):
        if c == SELF_CHUNK:
            return [(lo, hi) for lo, hi in ((0, SELF_BLOCK), (SELF_BLOCK + 1, BLOCKS)) if hi > lo]
        return [(0, BLOCKS)]

    def dispatch(c):
        def go(b, carry):
            pltpu.make_async_remote_copy(
                send.at[c, b], recv.at[c, b], send_sem.at[c], recv_sem.at[c],
                device_id=target(c, b, 1), device_id_type=MESH,
            ).start()
            return carry

        for lo, hi in spans(c):
            lax.fori_loop(lo, hi, go, 0)
        if c == SELF_CHUNK:
            pltpu.make_async_copy(
                send.at[c, SELF_BLOCK], recv.at[c, SELF_BLOCK], self_sem.at[0]
            ).start()

    def await_all(buffer, c, sem):
        count = BLOCKS - (c == SELF_CHUNK)
        part = buffer.at[c, pl.ds(0, count)]
        pltpu.make_async_copy(part, part, sem.at[c]).wait()

    gather(0)
    pl.semaphore_wait(bar, EXPERTS)
    dispatch(0)
    for c in range(1, CHUNKS):
        gather(c)
        dispatch(c)

    codes = jnp.concatenate([code0, code1, jnp.zeros((TOK - 2, TOK), I32)], axis=0)
    colcode[...] = jnp.transpose(codes.astype(F32))
    out_row = iota((256, 256), 0)
    in_row = ((out_row // 4) % 16) * 16 + (out_row // 64) * 4 + out_row % 4
    perm[0] = jnp.where(in_row == iota((256, 256), 1), 1.0, 0.0).astype(BF16)
    out_col = iota((256, 256), 1)
    in_col = ((out_col // 4) % 16) * 16 + (out_col // 64) * 4 + out_col % 4
    perm[1] = jnp.where(in_col == iota((256, 256), 0), 1.0, 0.0).astype(BF16)
    load_in.wait()
    load_out.wait()

    for c in range(CHUNKS):
        await_all(recv, c, recv_sem)
        if c == SELF_CHUNK:
            pltpu.make_async_copy(
                send.at[c, SELF_BLOCK], recv.at[c, SELF_BLOCK], self_sem.at[0]
            ).wait()
        base = c * SLOTS
        for g in range(2):
            packed = recv[c, g * 16:(g + 1) * 16].reshape(256, HALF)
            sorted_rows = dot(perm[0], packed, plain).astype(BF16)
            at = slice(base + g * 64, base + (g + 1) * 64)
            xrows[at, 0:HALF] = sorted_rows[0:64]
            xrows[at, HALF:] = sorted_rows[64:128]
            gorows[at, 0:HALF] = sorted_rows[128:192]
            gorows[at, HALF:] = sorted_rows[192:256]
        rows = slice(base, base + SLOTS)
        pre = dot(xrows[rows], win[...], plain)
        grad_act = dot(gorows[rows], wout[...], ((1,), (1,)))
        act, slope = gelu_parts(pre)
        act = act.astype(BF16)
        actrows[rows] = act
        grad_pre = (grad_act * slope).astype(BF16)
        gprows[rows] = grad_pre
        score = jnp.sum(act.astype(F32) * grad_act, axis=1, keepdims=True)
        spread = jnp.where(iota((SLOTS, 128), 0) % CAP == iota((SLOTS, 128), 1), score, 0.0)
        high = spread.astype(BF16)
        low = (spread - high.astype(F32)).astype(BF16)
        group = jnp.where(
            iota((BLOCKS, SLOTS), 1) // CAP == iota((BLOCKS, SLOTS), 0), 1.0, 0.0
        ).astype(BF16)
        score_ret[c] = (dot(group, high, plain) + dot(group, low, plain)).reshape(BLOCKS, 1, 128)
        grad_rows = dot(grad_pre, win[...], ((1,), (1,))).astype(BF16)
        for g in range(2):
            part = grad_rows[g * 64:(g + 1) * 64]
            stack = jnp.concatenate([part[:, q * 256:(q + 1) * 256] for q in range(4)], axis=0)
            mixed = dot(perm[1], stack, plain).astype(BF16)
            ret[c, g * 16:(g + 1) * 16] = mixed.reshape(16, 16, 256)

        def give(b, carry, c=c):
            to = target(c, b, -1)
            pltpu.make_async_remote_copy(
                ret.at[c, b], back.at[c, b], ret_sem.at[c], back_sem.at[c],
                device_id=to, device_id_type=MESH,
            ).start()
            pltpu.make_async_remote_copy(
                score_ret.at[c, b], score_back.at[c, b], sret_sem.at[c], sback_sem.at[c],
                device_id=to, device_id_type=MESH,
            ).start()
            return carry

        for lo, hi in spans(c):
            lax.fori_loop(lo, hi, give, 0)
        if c == SELF_CHUNK:
            pltpu.make_async_copy(
                ret.at[c, SELF_BLOCK], back.at[c, SELF_BLOCK], self_sem.at[1]
            ).start()
            pltpu.make_async_copy(
                score_ret.at[c, SELF_BLOCK], score_back.at[c, SELF_BLOCK], self_sem.at[2]
            ).start()

    theirs = pl.multiple_of((1 - rep) * HALF, HALF)
    mine = pl.multiple_of(rep * HALF, HALF)
    down = ((0,), (0,))
    wg_send[0] = dot(xrows[...], gprows[:, pl.ds(theirs, HALF)], down).astype(BF16)
    wg_send[1] = dot(actrows[...], gorows[:, pl.ds(theirs, HALF)], down).astype(BF16)
    swap = pltpu.make_async_remote_copy(
        wg_send, wg_recv, wgs_sem, wgr_sem, device_id=(1 - rep, me), device_id_type=MESH
    )
    swap.start()
    own_in = dot(xrows[...], gprows[:, pl.ds(mine, HALF)], down)
    own_out = dot(actrows[...], gorows[:, pl.ds(mine, HALF)], down)
    swap.wait()
    gwin_ref[0] = (own_in + wg_recv[0].astype(F32)).astype(BF16)
    gwout_ref[0] = (own_out + wg_recv[1].astype(F32)).astype(BF16)

    col0 = colcode[:, 0:1].astype(I32)
    col1 = colcode[:, 1:2].astype(I32)
    for c in range(CHUNKS):
        await_all(back, c, back_sem)
        if c == SELF_CHUNK:
            pltpu.make_async_copy(
                ret.at[c, SELF_BLOCK], back.at[c, SELF_BLOCK], self_sem.at[1]
            ).wait()
        lane = iota((TOK, ROWS), 1) + c * ROWS
        landed = back[c].reshape(ROWS, 256)
        for q in range(4):
            pick = jnp.where(lane == col0 + 4 * q, 1.0, jnp.where(lane == col1 + 4 * q, 1.0, 0.0))
            part = dot(pick.astype(BF16), landed, plain)
            if c == 0:
                total[:, q * 256:(q + 1) * 256] = part
            else:
                total[:, q * 256:(q + 1) * 256] += part
    gtok_ref[...] = total[...].astype(BF16)
    for c in range(CHUNKS):
        await_all(score_back, c, sback_sem)
    pltpu.make_async_copy(
        score_ret.at[SELF_CHUNK, SELF_BLOCK], score_back.at[SELF_CHUNK, SELF_BLOCK], self_sem.at[2]
    ).wait()
    scores = score_back[...].reshape(EXPERTS, 128)
    got0 = jnp.zeros((1, TOK), F32)
    got1 = jnp.zeros((1, TOK), F32)
    for s in range(CAP):
        column = scores[:, s:s + 1]
        got0 = got0 + jnp.where(pos0 == s, jnp.sum(hot0 * column, axis=0, keepdims=True), 0.0)
        got1 = got1 + jnp.where(pos1 == s, jnp.sum(hot1 * column, axis=0, keepdims=True), 0.0)
    ggate_ref[...] = jnp.concatenate([got0, got1], axis=0) / gate_low

    for c in range(CHUNKS):
        await_all(send, c, send_sem)
        await_all(ret, c, ret_sem)
        await_all(score_ret, c, sret_sem)


def body(tokens, cotangent, gate_values, expert_ids, keep_second, weight_in, weight_out):
    vmem = pl.BlockSpec(memory_space=pltpu.VMEM)
    hbm = pl.BlockSpec(memory_space=pl.ANY)
    dma = pltpu.SemaphoreType.DMA
    flops = 2 * 512 * 1024 * 1024 * 6
    grad_tokens, grad_gates, grad_in, grad_out = pl.pallas_call(
        kernel,
        out_shape=(
            jax.ShapeDtypeStruct((TOK, D), BF16),
            jax.ShapeDtypeStruct((2, TOK), F32),
            jax.ShapeDtypeStruct((1, D, HALF), BF16),
            jax.ShapeDtypeStruct((1, F, HALF), BF16),
        ),
        in_specs=[vmem] * 5 + [hbm] * 2,
        out_specs=(vmem,) * 4,
        scratch_shapes=[
            pltpu.VMEM((D, F), BF16),
            pltpu.VMEM((F, D), BF16),
            pltpu.VMEM((512, HALF), BF16),
            pltpu.VMEM((CHUNKS, BLOCKS, 16, HALF), BF16),
            pltpu.VMEM((CHUNKS, BLOCKS, 16, HALF), BF16),
            pltpu.VMEM((CHUNKS, BLOCKS, 16, 256), BF16),
            pltpu.VMEM((CHUNKS, BLOCKS, 16, 256), BF16),
            pltpu.VMEM((CHUNKS, BLOCKS, 1, 128), F32),
            pltpu.VMEM((CHUNKS, BLOCKS, 1, 128), F32),
            pltpu.VMEM((512, D), BF16),
            pltpu.VMEM((512, D), BF16),
            pltpu.VMEM((512, F), BF16),
            pltpu.VMEM((512, F), BF16),
            pltpu.VMEM((2, 256, 256), BF16),
            pltpu.VMEM((2, D, HALF), BF16),
            pltpu.VMEM((2, D, HALF), BF16),
            pltpu.VMEM((TOK, TOK), F32),
            pltpu.VMEM((TOK, D), F32),
            dma((2,)), dma((3,)),
            dma((CHUNKS,)), dma((CHUNKS,)), dma((CHUNKS,)), dma((CHUNKS,)),
            dma((CHUNKS,)), dma((CHUNKS,)), dma, dma,
        ],
        compiler_params=pltpu.CompilerParams(
            collective_id=0, has_side_effects=True, vmem_limit_bytes=56 * 2**20
        ),
        cost_estimate=pl.CostEstimate(
            flops=flops, bytes_accessed=7 * 2**20, transcendentals=512 * 1024
        ),
    )(
        tokens,
        cotangent,
        gate_values.T,
        expert_ids.T,
        keep_second.reshape(1, TOK),
        weight_in,
        weight_out,
    )
    return grad_tokens, grad_gates.T, grad_in, grad_out


def solution(mesh):
    in_specs = (
        P(("rep", "expert"), None),
        P(("rep", "expert"), None),
        P(("rep", "expert"), None),
        P(("rep", "expert"), None),
        P(("rep", "expert")),
        P("expert", None, None),
        P("expert", None, None),
    )
    out_specs = (
        P(("rep", "expert"), None),
        P(("rep", "expert"), None),
        P("expert", None, "rep"),
        P("expert", None, "rep"),
    )
    return jax.shard_map(body, mesh=mesh, in_specs=in_specs, out_specs=out_specs, check_vma=False)
```

```python
import functools

import jax
import jax.numpy as jnp
from jax import lax
from jax.experimental import pallas as pl
from jax.experimental.pallas import tpu as pltpu
from jax.sharding import PartitionSpec as P

MESH = pl.DeviceIdType.MESH
F32, BF16, I32 = jnp.float32, jnp.bfloat16, jnp.int32
NZ, NY, NX = 8, 4, 4
PLANE = NY * NX
EXPERTS = NZ * PLANE
CAP = 4
TOK = 128
D = 1024
F = 1024
HALF = 512
ORDER = (0, 4, 3, 5, 2, 6, 1, 7)
CHUNKS = 4
BLOCKS = EXPERTS // CHUNKS
ROWS = BLOCKS * 16
SLOTS = BLOCKS * CAP
RUNS = (
    ((0, 16, 0, 0), (16, 24, 1, 3), (24, 32, 2, -3)),
    ((0, 16, 1, 2), (16, 32, 2, -2)),
    ((0, 16, 1, 1), (16, 32, 2, -1)),
    ((0, 16, 1, 0), (16, 32, 2, 0)),
)
STAY = ((0, 0), (3, 0), (3, 16))


def dot(a, b, contract):
    return lax.dot_general(a, b, (contract, ((), ())), preferred_element_type=F32)


def iota(shape, dim):
    return lax.broadcasted_iota(I32, shape, dim)


def gelu_parts(pre):
    const = 0.7978845608028654
    square = pre * pre
    inner = jnp.tanh(const * (pre + 0.044715 * square * pre))
    half = 0.5 * (1.0 + inner)
    slope = half + 0.5 * pre * (1.0 - inner * inner) * (
        const * (1.0 + 3.0 * 0.044715 * square)
    )
    return pre * half, slope


def kernel(
    tokens_hbm, cot_hbm, gates_hbm, ids_hbm, keep_hbm, win_hbm, wout_hbm,
    gtok_ref, ggate_ref, gwin_ref, gwout_ref,
    win, wout, win_t, wout_t, gates, ids_in, keep, xcat, xnear, meta, meta_near, send, recv, ret, back,
    score_ret, score_back, xrows, gorows, actrows, gprows, perm, wg_send, wg_recv,
    colcode, total, part_send, part_recv, score_send, score_recv,
    load_sem, near_send, near_recv, stay_sem, send_sem, recv_sem, ret_sem, back_sem,
    sret_sem, sback_sem, part_ssem, part_rsem, wgs_sem, wgr_sem,
):
    me = lax.axis_index("expert")
    rep = lax.axis_index("rep")
    my_z, my_y, my_x = me // PLANE, (me // NX) % NY, me % NX

    def device(dz, dy, dx):
        return (
            rep,
            ((my_z + dz + NZ) % NZ) * PLANE
            + ((my_y + dy + NY) % NY) * NX
            + (my_x + dx + NX) % NX,
        )

    def near(side):
        return device(1 - 2 * side, 0, 0)

    loads = [
        pltpu.make_async_copy(ids_hbm, ids_in, load_sem.at[0]),
        pltpu.make_async_copy(gates_hbm, gates, load_sem.at[1]),
        pltpu.make_async_copy(keep_hbm, keep, load_sem.at[2]),
        pltpu.make_async_copy(tokens_hbm.at[:, 0:HALF], xcat.at[0:128], load_sem.at[3]),
        pltpu.make_async_copy(tokens_hbm.at[:, HALF:D], xcat.at[128:256], load_sem.at[4]),
        pltpu.make_async_copy(cot_hbm.at[:, 0:HALF], xcat.at[256:384], load_sem.at[5]),
        pltpu.make_async_copy(cot_hbm.at[:, HALF:D], xcat.at[384:512], load_sem.at[6]),
        pltpu.make_async_copy(win_hbm.at[0], win, load_sem.at[7]),
        pltpu.make_async_copy(wout_hbm.at[0], wout, load_sem.at[8]),
    ]
    for load in loads[:7]:
        load.start()

    bar = pltpu.get_barrier_semaphore()

    def greet(i, carry):
        to = device(i // PLANE - 3, (i // NX) % NY, i % NX)
        pl.semaphore_signal(bar, inc=1, device_id=to, device_id_type=MESH)
        return carry

    lax.fori_loop(0, 3 * PLANE, greet, 0)
    lax.fori_loop(3 * PLANE + 1, 7 * PLANE, greet, 0)
    pl.semaphore_signal(bar, inc=1, device_id=(1 - rep, me), device_id_type=MESH)
    for load in loads[7:]:
        load.start()

    for load in loads[:3]:
        load.wait()
    ids = ids_in[...]
    dz = (ids // PLANE - my_z + NZ) % NZ
    dy = ((ids // NX) % NY - my_y + NY) % NY
    dx = (ids % NX - my_x + NX) % NX
    pz = jnp.zeros_like(dz)
    for at, off in enumerate(ORDER):
        pz = jnp.where(dz == off, at, pz)
    place = pz * PLANE + dy * NX + dx
    first, second = place[0:1], place[1:2]
    hot0 = jnp.where(iota((EXPERTS, TOK), 0) == first, 1.0, 0.0)
    hot1 = jnp.where(iota((EXPERTS, TOK), 0) == second, 1.0, 0.0)
    upper = jnp.where(iota((TOK, TOK), 0) < iota((TOK, TOK), 1), 1.0, 0.0).astype(BF16)
    plain = ((1,), (0,))
    before0 = dot(hot0.astype(BF16), upper, plain)
    before1 = dot(hot1.astype(BF16), upper, plain) + jnp.sum(hot0, axis=1, keepdims=True)
    pos0 = jnp.sum(hot0 * before0, axis=0, keepdims=True)
    pos1 = jnp.sum(hot1 * before1, axis=0, keepdims=True)
    gate_low = gates[...].astype(BF16).astype(F32)
    meta[...] = jnp.concatenate(
        [
            first.astype(F32) * 16 + pos0,
            second.astype(F32) * 16 + pos1,
            gate_low[0:1],
            gate_low[1:2] * keep[...].astype(F32),
            jnp.zeros((4, TOK), F32),
        ],
        axis=0,
    )

    def hand_over(side):
        to = near(side)
        return [
            pltpu.make_async_remote_copy(
                meta, meta_near.at[side], near_send.at[side, 0], near_recv.at[side, 0],
                device_id=to, device_id_type=MESH,
            )
        ] + [
            pltpu.make_async_remote_copy(
                xcat.at[part * 256:(part + 1) * 256],
                xnear.at[side, part * 256:(part + 1) * 256],
                near_send.at[side, 1 + part], near_recv.at[side, 1 + part],
                device_id=to, device_id_type=MESH,
            )
            for part in range(2)
        ]

    handed = [hand_over(0), hand_over(1)]
    for load in loads[3:7]:
        load.wait()
    pl.semaphore_wait(bar, 7 * PLANE)
    for part in range(3):
        for side in range(2):
            handed[side][part].start()

    def quads(source):
        rows = meta[...] if source == 0 else meta_near[source - 1]
        code0, code1 = rows[0:1].astype(I32), rows[1:2].astype(I32)
        one = jnp.ones((1, TOK), F32)
        return (
            jnp.concatenate([code0 + 4 * q for q in range(4)], axis=1),
            jnp.concatenate([code1 + 4 * q for q in range(4)], axis=1),
            jnp.concatenate([one, one, rows[2:3], rows[2:3]], axis=1),
            jnp.concatenate([one, one, rows[3:4], rows[3:4]], axis=1),
        )

    def gather(c, run, quad):
        lo, hi, source, _ = run
        row = iota(((hi - lo) * 16, 512), 0) + (c * BLOCKS + lo) * 16
        pick = jnp.where(row == quad[0], quad[2], jnp.where(row == quad[1], quad[3], 0.0))
        held = xcat[...] if source == 0 else xnear[source - 1]
        block = dot(pick.astype(BF16), held, plain).astype(BF16)
        send[c, lo:hi] = block.reshape(hi - lo, 16, HALF)

    def target(b, off, sign):
        return device(sign * off, sign * ((b // NX) % NY), sign * (b % NX))

    def each(c, run, step):
        lo, hi = run[:2]
        lax.fori_loop(lo + ((c, lo) in STAY), hi, step, 0)

    def dispatch(c, run):
        def go(b, carry):
            pltpu.make_async_remote_copy(
                send.at[c, b], recv.at[c, b], send_sem.at[c], recv_sem.at[c],
                device_id=target(b, run[3], 1), device_id_type=MESH,
            ).start()
            return carry

        each(c, run, go)

    def stay(sources, results, kind, c):
        return [
            pltpu.make_async_copy(sources.at[c, b], results.at[c, b], stay_sem.at[kind, i])
            for i, (at, b) in enumerate(STAY)
            if at == c
        ]

    def await_all(buffer, c, sem):
        count = BLOCKS - sum(at == c for at, _ in STAY)
        part = buffer.at[c, pl.ds(0, count)]
        pltpu.make_async_copy(part, part, sem.at[c]).wait()

    own = quads(0)
    gather(0, RUNS[0][0], own)
    dispatch(0, RUNS[0][0])
    for copy in stay(send, recv, 0, 0):
        copy.start()

    def column_codes(source):
        rows = meta[...] if source == 0 else meta_near[source - 1]
        tall = jnp.concatenate([rows, jnp.zeros((TOK - 8, TOK), F32)], axis=0)
        colcode[source] = jnp.transpose(tall)

    column_codes(0)
    out_row = iota((256, 256), 0)
    in_row = ((out_row // 4) % 16) * 16 + (out_row // 64) * 4 + out_row % 4
    perm[0] = jnp.where(in_row == iota((256, 256), 1), 1.0, 0.0).astype(BF16)
    out_col = iota((256, 256), 1)
    in_col = ((out_col // 4) % 16) * 16 + (out_col // 64) * 4 + out_col % 4
    perm[1] = jnp.where(in_col == iota((256, 256), 0), 1.0, 0.0).astype(BF16)

    for load in loads[7:]:
        load.wait()
    for r in range(0, D, 256):
        win_t[:, r:r + 256] = jnp.transpose(win[r:r + 256, :])
        wout_t[:, r:r + 256] = jnp.transpose(wout[r:r + 256, :])
    for side in range(2):
        handed[side][0].wait_recv()
    column_codes(1)
    column_codes(2)
    quad = [own, quads(1), quads(2)]
    for part in (1, 2):
        for side in range(2):
            handed[side][part].wait_recv()
    for c in range(CHUNKS):
        for run in RUNS[c]:
            if run[2] > 0:
                gather(c, run, quad[run[2]])
                dispatch(c, run)
        if c > 0:
            for copy in stay(send, recv, 0, c):
                copy.start()

    for c in range(CHUNKS):
        await_all(recv, c, recv_sem)
        for copy in stay(send, recv, 0, c):
            copy.wait()
        base = c * SLOTS
        for g in range(2):
            packed = recv[c, g * 16:(g + 1) * 16].reshape(256, HALF)
            sorted_rows = dot(perm[0], packed, plain).astype(BF16)
            at = slice(base + g * 64, base + (g + 1) * 64)
            xrows[at, 0:HALF] = sorted_rows[0:64]
            xrows[at, HALF:] = sorted_rows[64:128]
            gorows[at, 0:HALF] = sorted_rows[128:192]
            gorows[at, HALF:] = sorted_rows[192:256]
        rows = slice(base, base + SLOTS)
        pre = dot(xrows[rows], win[...], plain)
        grad_act = dot(gorows[rows], wout_t[...], plain)
        act, slope = gelu_parts(pre)
        act = act.astype(BF16)
        actrows[rows] = act
        grad_pre = (grad_act * slope).astype(BF16)
        gprows[rows] = grad_pre
        score = jnp.sum(act.astype(F32) * grad_act, axis=1, keepdims=True)
        spread = jnp.where(iota((SLOTS, 128), 0) % CAP == iota((SLOTS, 128), 1), score, 0.0)
        high = spread.astype(BF16)
        low = (spread - high.astype(F32)).astype(BF16)
        group = jnp.where(
            iota((BLOCKS, SLOTS), 1) // CAP == iota((BLOCKS, SLOTS), 0), 1.0, 0.0
        ).astype(BF16)
        score_ret[c] = (dot(group, high, plain) + dot(group, low, plain)).reshape(BLOCKS, 1, 128)
        grad_rows = dot(grad_pre, win_t[...], plain).astype(BF16)
        for g in range(2):
            piece = grad_rows[g * 64:(g + 1) * 64]
            stack = jnp.concatenate([piece[:, q * 256:(q + 1) * 256] for q in range(4)], axis=0)
            mixed = dot(perm[1], stack, plain).astype(BF16)
            ret[c, g * 16:(g + 1) * 16] = mixed.reshape(16, 16, 256)

        for run in RUNS[c]:
            def give(b, carry, c=c, run=run):
                to = target(b, run[3], -1)
                pltpu.make_async_remote_copy(
                    ret.at[c, b], back.at[c, b], ret_sem.at[c], back_sem.at[c],
                    device_id=to, device_id_type=MESH,
                ).start()
                pltpu.make_async_remote_copy(
                    score_ret.at[c, b], score_back.at[c, b], sret_sem.at[c], sback_sem.at[c],
                    device_id=to, device_id_type=MESH,
                ).start()
                return carry

            each(c, run, give)
        for copy in stay(ret, back, 1, c) + stay(score_ret, score_back, 2, c):
            copy.start()

    theirs = pl.multiple_of((1 - rep) * HALF, HALF)
    mine = pl.multiple_of(rep * HALF, HALF)
    down = ((0,), (0,))
    wg_send[0] = dot(xrows[...], gprows[:, pl.ds(theirs, HALF)], down).astype(BF16)
    wg_send[1] = dot(actrows[...], gorows[:, pl.ds(theirs, HALF)], down).astype(BF16)
    swap = pltpu.make_async_remote_copy(
        wg_send, wg_recv, wgs_sem, wgr_sem, device_id=(1 - rep, me), device_id_type=MESH
    )
    swap.start()

    started = set()
    for c in range(CHUNKS):
        await_all(back, c, back_sem)
        for copy in stay(ret, back, 1, c):
            copy.wait()
        for lo, hi, source, _ in RUNS[c]:
            size = (hi - lo) * 16
            lane = iota((TOK, size), 1) + (c * BLOCKS + lo) * 16
            landed = back[c, lo:hi].reshape(size, 256)
            col0 = colcode[source, :, 0:1].astype(I32)
            col1 = colcode[source, :, 1:2].astype(I32)
            for q in range(4):
                pick = jnp.where(
                    lane == col0 + 4 * q, 1.0, jnp.where(lane == col1 + 4 * q, 1.0, 0.0)
                )
                piece = dot(pick.astype(BF16), landed, plain)
                where = slice(q * 256, (q + 1) * 256)
                if source in started:
                    piece = piece + total[source, :, where]
                if c == CHUNKS - 1:
                    part_send[source - 1, :, where] = piece.astype(BF16)
                else:
                    total[source, :, where] = piece
            started.add(source)
            if c == CHUNKS - 1:
                pltpu.make_async_remote_copy(
                    part_send.at[source - 1], part_recv.at[source - 1],
                    part_ssem.at[source - 1, 0], part_rsem.at[source - 1, 0],
                    device_id=near(2 - source), device_id_type=MESH,
                ).start()

    for c in range(CHUNKS):
        await_all(score_back, c, sback_sem)
        for copy in stay(score_ret, score_back, 2, c):
            copy.wait()
    scores = score_back[...].reshape(EXPERTS, 128)
    spot = iota((EXPERTS, TOK), 0)
    low_half = spot % BLOCKS < 16

    def score_rows(source):
        rows = meta[...] if source == 0 else meta_near[source - 1]
        if source == 0:
            here = spot < 16
        elif source == 1:
            here = ((spot >= BLOCKS) & low_half) | ((spot >= 16) & (spot < 24))
        else:
            here = ((spot >= BLOCKS) & jnp.logical_not(low_half)) | ((spot >= 24) & (spot < BLOCKS))
        found = []
        for k in range(2):
            code = rows[k:k + 1].astype(I32)
            hot = jnp.where((spot == code // 16) & here, 1.0, 0.0)
            got = jnp.zeros((1, TOK), F32)
            for s in range(CAP):
                hit = jnp.sum(hot * scores[:, s:s + 1], axis=0, keepdims=True)
                got = got + jnp.where(code % 16 == s, hit, 0.0)
            found.append(got)
        return jnp.concatenate(found + [jnp.zeros((6, TOK), F32)], axis=0)

    for source in (1, 2):
        score_send[source - 1] = score_rows(source)
        pltpu.make_async_remote_copy(
            score_send.at[source - 1], score_recv.at[source - 1],
            part_ssem.at[source - 1, 1], part_rsem.at[source - 1, 1],
            device_id=near(2 - source), device_id_type=MESH,
        ).start()
    own_scores = score_rows(0)

    own_in = dot(xrows[...], gprows[:, pl.ds(mine, HALF)], down)
    own_out = dot(actrows[...], gorows[:, pl.ds(mine, HALF)], down)
    swap.wait()
    gwin_ref[0] = (own_in + wg_recv[0].astype(F32)).astype(BF16)
    gwout_ref[0] = (own_out + wg_recv[1].astype(F32)).astype(BF16)

    for side in range(2):
        for kind, (sent, landed) in enumerate(((part_send, part_recv), (score_send, score_recv))):
            pltpu.make_async_remote_copy(
                sent.at[side], landed.at[side], part_ssem.at[side, kind], part_rsem.at[side, kind],
                device_id=near(1 - side), device_id_type=MESH,
            ).wait()
    gtok_ref[...] = (
        total[0] + part_recv[0].astype(F32) + part_recv[1].astype(F32)
    ).astype(BF16)
    all_scores = own_scores + score_recv[0] + score_recv[1]
    ggate_ref[...] = all_scores[0:2] / gate_low

    for side in range(2):
        for part in range(3):
            handed[side][part].wait_send()
    for c in range(CHUNKS):
        await_all(send, c, send_sem)
        await_all(ret, c, ret_sem)
        await_all(score_ret, c, sret_sem)


def finish(*refs):
    sources, results, sems = refs[:4], refs[4:8], refs[8]
    for i in range(4):
        pltpu.make_async_copy(sources[i], results[i], sems.at[i]).start()
    for i in range(4):
        pltpu.make_async_copy(sources[i], results[i], sems.at[i]).wait()


def body(tokens, cotangent, gate_values, expert_ids, keep_second, weight_in, weight_out):
    vmem = pl.BlockSpec(memory_space=pltpu.VMEM)
    hbm = pl.BlockSpec(memory_space=pl.ANY)
    dma = pltpu.SemaphoreType.DMA
    parts = pl.pallas_call(
        kernel,
        out_shape=(
            pltpu.VMEM((TOK, D), BF16),
            pltpu.VMEM((2, TOK), F32),
            pltpu.VMEM((1, D, HALF), BF16),
            pltpu.VMEM((1, F, HALF), BF16),
        ),
        in_specs=[hbm] * 7,
        out_specs=(vmem,) * 4,
        scratch_shapes=[
            pltpu.VMEM((D, F), BF16),
            pltpu.VMEM((F, D), BF16),
            pltpu.VMEM((F, D), BF16),
            pltpu.VMEM((D, F), BF16),
            pltpu.VMEM((2, TOK), F32),
            pltpu.VMEM((2, TOK), I32),
            pltpu.VMEM((1, TOK), I32),
            pltpu.VMEM((512, HALF), BF16),
            pltpu.VMEM((2, 512, HALF), BF16),
            pltpu.VMEM((8, TOK), F32),
            pltpu.VMEM((2, 8, TOK), F32),
            pltpu.VMEM((CHUNKS, BLOCKS, 16, HALF), BF16),
            pltpu.VMEM((CHUNKS, BLOCKS, 16, HALF), BF16),
            pltpu.VMEM((CHUNKS, BLOCKS, 16, 256), BF16),
            pltpu.VMEM((CHUNKS, BLOCKS, 16, 256), BF16),
            pltpu.VMEM((CHUNKS, BLOCKS, 1, 128), F32),
            pltpu.VMEM((CHUNKS, BLOCKS, 1, 128), F32),
            pltpu.VMEM((512, D), BF16),
            pltpu.VMEM((512, D), BF16),
            pltpu.VMEM((512, F), BF16),
            pltpu.VMEM((512, F), BF16),
            pltpu.VMEM((2, 256, 256), BF16),
            pltpu.VMEM((2, D, HALF), BF16),
            pltpu.VMEM((2, D, HALF), BF16),
            pltpu.VMEM((3, TOK, TOK), F32),
            pltpu.VMEM((3, TOK, D), F32),
            pltpu.VMEM((2, TOK, D), BF16),
            pltpu.VMEM((2, TOK, D), BF16),
            pltpu.VMEM((2, 8, TOK), F32),
            pltpu.VMEM((2, 8, TOK), F32),
            dma((9,)), dma((2, 3)), dma((2, 3)), dma((3, 3)),
            dma((CHUNKS,)), dma((CHUNKS,)), dma((CHUNKS,)), dma((CHUNKS,)),
            dma((CHUNKS,)), dma((CHUNKS,)), dma((2, 2)), dma((2, 2)), dma, dma,
        ],
        compiler_params=pltpu.CompilerParams(
            collective_id=0, has_side_effects=True, vmem_limit_bytes=60 * 2**20
        ),
        cost_estimate=pl.CostEstimate(
            flops=2 * 512 * 1024 * 1024 * 6, bytes_accessed=7 * 2**20, transcendentals=512 * 1024
        ),
    )(
        tokens,
        cotangent,
        gate_values.T,
        expert_ids.T,
        keep_second.reshape(1, TOK),
        weight_in,
        weight_out,
    )
    grad_tokens, grad_gates, grad_in, grad_out = pl.pallas_call(
        finish,
        out_shape=tuple(jax.ShapeDtypeStruct(p.shape, p.dtype) for p in parts),
        in_specs=[vmem] * 4,
        out_specs=(hbm,) * 4,
        scratch_shapes=[dma((4,))],
    )(*(pltpu.with_memory_space_constraint(p, pltpu.VMEM) for p in parts))
    return grad_tokens, grad_gates.T, grad_in, grad_out


def solution(mesh):
    in_specs = (
        P(("rep", "expert"), None),
        P(("rep", "expert"), None),
        P(("rep", "expert"), None),
        P(("rep", "expert"), None),
        P(("rep", "expert")),
        P("expert", None, None),
        P("expert", None, None),
    )
    out_specs = (
        P(("rep", "expert"), None),
        P(("rep", "expert"), None),
        P("expert", None, "rep"),
        P("expert", None, "rep"),
    )
    return jax.shard_map(body, mesh=mesh, in_specs=in_specs, out_specs=out_specs, check_vma=False)
```

```python
import functools

import jax
import jax.numpy as jnp
from jax import lax
from jax.experimental import pallas as pl
from jax.experimental.pallas import tpu as pltpu
from jax.sharding import PartitionSpec as P

MESH = pl.DeviceIdType.MESH
F32, BF16, I32 = jnp.float32, jnp.bfloat16, jnp.int32
NZ, NY, NX = 8, 4, 4
PLANE = NY * NX
EXPERTS = NZ * PLANE
CAP = 4
TOK = 128
D = 1024
F = 1024
HALF = 512
QUARTER = 256
ORDER = (0, 4, 3, 5, 2, 6, 1, 7)
CHUNKS = 4
BLOCKS = EXPERTS // CHUNKS
ROWS = BLOCKS * 16
SLOTS = BLOCKS * CAP
RUNS = (
    ((0, 16, 0, 0), (16, 24, 1, 3), (24, 32, 2, -3)),
    ((0, 16, 1, 2), (16, 32, 2, -2)),
    ((0, 16, 1, 1), (16, 32, 2, -1)),
    ((0, 16, 1, 0), (16, 32, 2, 0)),
)
FIRST = (0, 1, 2, 3)
STAY = ((0, 0), (3, 0), (3, 16))


def dot(a, b, contract):
    return lax.dot_general(a, b, (contract, ((), ())), preferred_element_type=F32)


def iota(shape, dim):
    return lax.broadcasted_iota(I32, shape, dim)


def gelu_parts(pre):
    const = 0.7978845608028654
    square = pre * pre
    inner = jnp.tanh(const * (pre + 0.044715 * square * pre))
    half = 0.5 * (1.0 + inner)
    slope = half + 0.5 * pre * (1.0 - inner * inner) * (
        const * (1.0 + 3.0 * 0.044715 * square)
    )
    return pre * half, slope


def kernel(
    tokens_hbm, cot_hbm, gates_hbm, ids_hbm, keep_hbm, win_hbm, wout_hbm,
    gtok_ref, ggate_ref, gwin_ref, gwout_ref,
    win, wout, win_t, wout_t, gates, ids_in, keep, xcat, xnear, meta, meta_near, send, recv, ret, back,
    score_ret, score_back, xrows, gorows, actrows, gprows, perm, wg_send, wg_recv,
    colcode, total, part_send, part_recv, score_send, score_recv,
    met_sem, load_sem, near_send, near_recv, stay_sem, send_sem, recv_sem, ret_sem, back_sem,
    sret_sem, sback_sem, part_ssem, part_rsem, wgs_sem, wgr_sem,
):
    me = lax.axis_index("expert")
    rep = lax.axis_index("rep")
    my_z, my_y, my_x = me // PLANE, (me // NX) % NY, me % NX

    def device(dz, dy, dx):
        return (
            rep,
            ((my_z + dz + NZ) % NZ) * PLANE
            + ((my_y + dy + NY) % NY) * NX
            + (my_x + dx + NX) % NX,
        )

    def near(side):
        return device(1 - 2 * side, 0, 0)

    loads = [
        pltpu.make_async_copy(ids_hbm, ids_in, load_sem.at[0]),
        pltpu.make_async_copy(gates_hbm, gates, load_sem.at[1]),
        pltpu.make_async_copy(keep_hbm, keep, load_sem.at[2]),
        pltpu.make_async_copy(win_hbm.at[0], win, load_sem.at[3]),
        pltpu.make_async_copy(wout_hbm.at[0], wout, load_sem.at[4]),
    ]
    row_loads = [
        [
            pltpu.make_async_copy(
                held.at[:, q * QUARTER:(q + 1) * QUARTER],
                xcat.at[kind, q * TOK:(q + 1) * TOK],
                load_sem.at[5 + 4 * kind + q],
            )
            for q in range(4)
        ]
        for kind, held in enumerate((tokens_hbm, cot_hbm))
    ]
    for load in row_loads[0] + loads[:3] + row_loads[1]:
        load.start()

    bar = pltpu.get_barrier_semaphore()

    beside = [[device(*(step * (axis == a) for a in range(3))) for step in (1, -1)] for axis in range(3)]
    for to in [to for pair in beside for to in pair] + [(1 - rep, me)]:
        pl.semaphore_signal(bar, inc=1, device_id=to, device_id_type=MESH)
    for load in loads[3:]:
        load.start()

    def know(axis, at):
        for to in beside[axis]:
            pl.semaphore_signal(met_sem.at[at], inc=1, device_id=to, device_id_type=MESH)
        pl.semaphore_wait(met_sem.at[at], 2)

    def hand_over(side):
        to = near(side)
        return [
            pltpu.make_async_remote_copy(
                meta, meta_near.at[side], near_send.at[side, 2], near_recv.at[side, 2],
                device_id=to, device_id_type=MESH,
            ) if kind == 2 else pltpu.make_async_remote_copy(
                xcat.at[kind], xnear.at[side, kind],
                near_send.at[side, kind], near_recv.at[side, kind],
                device_id=to, device_id_type=MESH,
            )
            for kind in range(3)
        ]

    handed = [hand_over(0), hand_over(1)]
    for load in row_loads[0]:
        load.wait()
    pl.semaphore_wait(bar, 7)
    for side in range(2):
        handed[side][0].start()

    for load in loads[:3]:
        load.wait()
    ids = ids_in[...]
    dz = (ids // PLANE - my_z + NZ) % NZ
    dy = ((ids // NX) % NY - my_y + NY) % NY
    dx = (ids % NX - my_x + NX) % NX
    pz = jnp.zeros_like(dz)
    for at, off in enumerate(ORDER):
        pz = jnp.where(dz == off, at, pz)
    place = pz * PLANE + dy * NX + dx
    first, second = place[0:1], place[1:2]
    hot0 = jnp.where(iota((EXPERTS, TOK), 0) == first, 1.0, 0.0)
    hot1 = jnp.where(iota((EXPERTS, TOK), 0) == second, 1.0, 0.0)
    upper = jnp.where(iota((TOK, TOK), 0) < iota((TOK, TOK), 1), 1.0, 0.0).astype(BF16)
    plain = ((1,), (0,))
    before0 = dot(hot0.astype(BF16), upper, plain)
    before1 = dot(hot1.astype(BF16), upper, plain) + jnp.sum(hot0, axis=1, keepdims=True)
    pos0 = jnp.sum(hot0 * before0, axis=0, keepdims=True)
    pos1 = jnp.sum(hot1 * before1, axis=0, keepdims=True)
    gate_low = gates[...].astype(BF16).astype(F32)
    meta[...] = jnp.concatenate(
        [
            first.astype(F32) * 16 + pos0,
            second.astype(F32) * 16 + pos1,
            gate_low[0:1],
            gate_low[1:2] * keep[...].astype(F32),
            jnp.zeros((4, TOK), F32),
        ],
        axis=0,
    )

    for side in range(2):
        handed[side][2].start()
    for load in row_loads[1]:
        load.wait()
    for side in range(2):
        handed[side][1].start()

    def quads(source):
        rows = meta[...] if source == 0 else meta_near[source - 1]
        code0, code1 = rows[0:1].astype(I32), rows[1:2].astype(I32)
        return (
            jnp.concatenate([code0 + 4 * q for q in range(4)], axis=1),
            jnp.concatenate([code1 + 4 * q for q in range(4)], axis=1),
            jnp.concatenate([rows[2:3]] * 4, axis=1),
            jnp.concatenate([rows[3:4]] * 4, axis=1),
        )

    def gather(kind, c, run, quad):
        lo, hi, source, _ = run
        row = iota(((hi - lo) * 16, 512), 0) + (c * BLOCKS + lo) * 16
        one, two = (1.0, 1.0) if kind == 0 else quad[2:]
        pick = jnp.where(row == quad[0], one, jnp.where(row == quad[1], two, 0.0))
        held = xcat[kind] if source == 0 else xnear[source - 1, kind]
        block = dot(pick.astype(BF16), held, plain).astype(BF16)
        send[kind, c, lo:hi] = block.reshape(hi - lo, 16, QUARTER)

    def target(b, off, sign):
        return device(sign * off, sign * ((b // NX) % NY), sign * (b % NX))

    def each(c, run, step):
        lo, hi = run[:2]
        lax.fori_loop(lo + ((c, lo) in STAY), hi, step, 0)

    def dispatch(kind, c, run):
        def go(b, carry):
            pltpu.make_async_remote_copy(
                send.at[kind, c, b], recv.at[kind, c, b],
                send_sem.at[kind, c], recv_sem.at[kind, c],
                device_id=target(b, run[3], 1), device_id_type=MESH,
            ).start()
            return carry

        each(c, run, go)

    def stay(sources, results, kind, c):
        return [
            pltpu.make_async_copy(sources.at[c, b], results.at[c, b], stay_sem.at[kind, i])
            for i, (at, b) in enumerate(STAY)
            if at == c
        ]

    def await_all(buffer, c, sem):
        count = BLOCKS - sum(at == c for at, _ in STAY)
        part = buffer.at[c, pl.ds(0, count)]
        pltpu.make_async_copy(part, part, sem.at[c]).wait()

    def stay_rows(kind, c):
        return stay(send.at[kind], recv.at[kind], kind, c)

    know(2, 0)
    know(1, 1)
    know(1, 2)
    own = quads(0)
    for kind in range(2):
        gather(kind, 0, RUNS[0][0], own)
        dispatch(kind, 0, RUNS[0][0])
        for copy in stay_rows(kind, 0):
            copy.start()

    def column_codes(source):
        rows = meta[...] if source == 0 else meta_near[source - 1]
        tall = jnp.concatenate([rows, jnp.zeros((TOK - 8, TOK), F32)], axis=0)
        colcode[source] = jnp.transpose(tall)

    column_codes(0)
    out_row = iota((256, 256), 0)
    in_row = ((out_row // 4) % 16) * 16 + (out_row // 64) * 4 + out_row % 4
    perm[0] = jnp.where(in_row == iota((256, 256), 1), 1.0, 0.0).astype(BF16)
    out_col = iota((256, 256), 1)
    in_col = ((out_col // 4) % 16) * 16 + (out_col // 64) * 4 + out_col % 4
    perm[1] = jnp.where(in_col == iota((256, 256), 0), 1.0, 0.0).astype(BF16)

    know(0, 3)
    know(0, 4)
    know(0, 5)
    for load in loads[3:]:
        load.wait()
    for r in range(0, D, 256):
        win_t[:, r:r + 256] = jnp.transpose(win[r:r + 256, :])
        wout_t[:, r:r + 256] = jnp.transpose(wout[r:r + 256, :])
    for side in range(2):
        handed[side][2].wait_recv()
    column_codes(1)
    column_codes(2)
    quad = [own, quads(1), quads(2)]
    for kind, order in ((0, FIRST), (1, range(CHUNKS))):
        for side in range(2):
            handed[side][kind].wait_recv()
        for c in order:
            for run in RUNS[c]:
                if run[2] > 0:
                    gather(kind, c, run, quad[run[2]])
                    dispatch(kind, c, run)
            if c > 0:
                for copy in stay_rows(kind, c):
                    copy.start()

    for c in range(CHUNKS):
        base = c * SLOTS
        for kind, plain_rows in enumerate((xrows, gorows)):
            await_all(recv.at[kind], c, recv_sem.at[kind])
            for copy in stay_rows(kind, c):
                copy.wait()
            for g in range(2):
                packed = recv[kind, c, g * 16:(g + 1) * 16].reshape(256, QUARTER)
                sorted_rows = dot(perm[0], packed, plain).astype(BF16)
                at = slice(base + g * 64, base + (g + 1) * 64)
                for q in range(4):
                    plain_rows[at, q * QUARTER:(q + 1) * QUARTER] = sorted_rows[q * 64:(q + 1) * 64]
        rows = slice(base, base + SLOTS)
        pre = dot(xrows[rows], win[...], plain)
        grad_act = dot(gorows[rows], wout_t[...], plain)
        act, slope = gelu_parts(pre)
        act = act.astype(BF16)
        actrows[rows] = act
        grad_pre = (grad_act * slope).astype(BF16)
        gprows[rows] = grad_pre
        score = jnp.sum(act.astype(F32) * grad_act, axis=1, keepdims=True)
        spread = jnp.where(iota((SLOTS, 128), 0) % CAP == iota((SLOTS, 128), 1), score, 0.0)
        high = spread.astype(BF16)
        low = (spread - high.astype(F32)).astype(BF16)
        group = jnp.where(
            iota((BLOCKS, SLOTS), 1) // CAP == iota((BLOCKS, SLOTS), 0), 1.0, 0.0
        ).astype(BF16)
        score_ret[c] = (dot(group, high, plain) + dot(group, low, plain)).reshape(BLOCKS, 1, 128)
        grad_rows = dot(grad_pre, win_t[...], plain).astype(BF16)
        for g in range(2):
            piece = grad_rows[g * 64:(g + 1) * 64]
            stack = jnp.concatenate([piece[:, q * 256:(q + 1) * 256] for q in range(4)], axis=0)
            mixed = dot(perm[1], stack, plain).astype(BF16)
            ret[c, g * 16:(g + 1) * 16] = mixed.reshape(16, 16, 256)

        for run in RUNS[c]:
            def give(b, carry, c=c, run=run):
                to = target(b, run[3], -1)
                pltpu.make_async_remote_copy(
                    ret.at[c, b], back.at[c, b], ret_sem.at[c], back_sem.at[c],
                    device_id=to, device_id_type=MESH,
                ).start()
                pltpu.make_async_remote_copy(
                    score_ret.at[c, b], score_back.at[c, b], sret_sem.at[c], sback_sem.at[c],
                    device_id=to, device_id_type=MESH,
                ).start()
                return carry

            each(c, run, give)
        for copy in stay(ret, back, 2, c) + stay(score_ret, score_back, 3, c):
            copy.start()

    theirs = pl.multiple_of((1 - rep) * HALF, HALF)
    mine = pl.multiple_of(rep * HALF, HALF)
    down = ((0,), (0,))
    wg_send[0] = dot(xrows[...], gprows[:, pl.ds(theirs, HALF)], down).astype(BF16)
    wg_send[1] = dot(actrows[...], gorows[:, pl.ds(theirs, HALF)], down).astype(BF16)
    swap = pltpu.make_async_remote_copy(
        wg_send, wg_recv, wgs_sem, wgr_sem, device_id=(1 - rep, me), device_id_type=MESH
    )
    swap.start()

    started = set()
    for c in range(CHUNKS):
        await_all(back, c, back_sem)
        for copy in stay(ret, back, 2, c):
            copy.wait()
        for lo, hi, source, _ in RUNS[c]:
            size = (hi - lo) * 16
            lane = iota((TOK, size), 1) + (c * BLOCKS + lo) * 16
            landed = back[c, lo:hi].reshape(size, 256)
            col0 = colcode[source, :, 0:1].astype(I32)
            col1 = colcode[source, :, 1:2].astype(I32)
            for q in range(4):
                pick = jnp.where(
                    lane == col0 + 4 * q, 1.0, jnp.where(lane == col1 + 4 * q, 1.0, 0.0)
                )
                piece = dot(pick.astype(BF16), landed, plain)
                where = slice(q * 256, (q + 1) * 256)
                if source in started:
                    piece = piece + total[source, :, where]
                if c == CHUNKS - 1:
                    part_send[source - 1, :, where] = piece.astype(BF16)
                else:
                    total[source, :, where] = piece
            started.add(source)
            if c == CHUNKS - 1:
                pltpu.make_async_remote_copy(
                    part_send.at[source - 1], part_recv.at[source - 1],
                    part_ssem.at[source - 1, 0], part_rsem.at[source - 1, 0],
                    device_id=near(2 - source), device_id_type=MESH,
                ).start()

    for c in range(CHUNKS):
        await_all(score_back, c, sback_sem)
        for copy in stay(score_ret, score_back, 3, c):
            copy.wait()
    scores = score_back[...].reshape(EXPERTS, 128)
    spot = iota((EXPERTS, TOK), 0)
    low_half = spot % BLOCKS < 16

    def score_rows(source):
        rows = meta[...] if source == 0 else meta_near[source - 1]
        if source == 0:
            here = spot < 16
        elif source == 1:
            here = ((spot >= BLOCKS) & low_half) | ((spot >= 16) & (spot < 24))
        else:
            here = ((spot >= BLOCKS) & jnp.logical_not(low_half)) | ((spot >= 24) & (spot < BLOCKS))
        found = []
        for k in range(2):
            code = rows[k:k + 1].astype(I32)
            hot = jnp.where((spot == code // 16) & here, 1.0, 0.0)
            got = jnp.zeros((1, TOK), F32)
            for s in range(CAP):
                hit = jnp.sum(hot * scores[:, s:s + 1], axis=0, keepdims=True)
                got = got + jnp.where(code % 16 == s, hit, 0.0)
            found.append(got)
        return jnp.concatenate(found + [jnp.zeros((6, TOK), F32)], axis=0)

    for source in (1, 2):
        score_send[source - 1] = score_rows(source)
        pltpu.make_async_remote_copy(
            score_send.at[source - 1], score_recv.at[source - 1],
            part_ssem.at[source - 1, 1], part_rsem.at[source - 1, 1],
            device_id=near(2 - source), device_id_type=MESH,
        ).start()
    own_scores = score_rows(0)

    own_in = dot(xrows[...], gprows[:, pl.ds(mine, HALF)], down)
    own_out = dot(actrows[...], gorows[:, pl.ds(mine, HALF)], down)
    swap.wait()
    gwin_ref[0] = (own_in + wg_recv[0].astype(F32)).astype(BF16)
    gwout_ref[0] = (own_out + wg_recv[1].astype(F32)).astype(BF16)

    for side in range(2):
        for kind, (sent, landed) in enumerate(((part_send, part_recv), (score_send, score_recv))):
            pltpu.make_async_remote_copy(
                sent.at[side], landed.at[side], part_ssem.at[side, kind], part_rsem.at[side, kind],
                device_id=near(1 - side), device_id_type=MESH,
            ).wait()
    gtok_ref[...] = (
        total[0] + part_recv[0].astype(F32) + part_recv[1].astype(F32)
    ).astype(BF16)
    all_scores = own_scores + score_recv[0] + score_recv[1]
    ggate_ref[...] = all_scores[0:2] / gate_low

    for side in range(2):
        for part in range(3):
            handed[side][part].wait_send()
    for c in range(CHUNKS):
        for kind in range(2):
            await_all(send.at[kind], c, send_sem.at[kind])
        await_all(ret, c, ret_sem)
        await_all(score_ret, c, sret_sem)


def finish(*refs):
    sources, results, sems = refs[:4], refs[4:8], refs[8]
    for i in range(4):
        pltpu.make_async_copy(sources[i], results[i], sems.at[i]).start()
    for i in range(4):
        pltpu.make_async_copy(sources[i], results[i], sems.at[i]).wait()


def body(tokens, cotangent, gate_values, expert_ids, keep_second, weight_in, weight_out):
    vmem = pl.BlockSpec(memory_space=pltpu.VMEM)
    hbm = pl.BlockSpec(memory_space=pl.ANY)
    dma = pltpu.SemaphoreType.DMA
    parts = pl.pallas_call(
        kernel,
        out_shape=(
            pltpu.VMEM((TOK, D), BF16),
            pltpu.VMEM((2, TOK), F32),
            pltpu.VMEM((1, D, HALF), BF16),
            pltpu.VMEM((1, F, HALF), BF16),
        ),
        in_specs=[hbm] * 7,
        out_specs=(vmem,) * 4,
        scratch_shapes=[
            pltpu.VMEM((D, F), BF16),
            pltpu.VMEM((F, D), BF16),
            pltpu.VMEM((F, D), BF16),
            pltpu.VMEM((D, F), BF16),
            pltpu.VMEM((2, TOK), F32),
            pltpu.VMEM((2, TOK), I32),
            pltpu.VMEM((1, TOK), I32),
            pltpu.VMEM((2, 512, QUARTER), BF16),
            pltpu.VMEM((2, 2, 512, QUARTER), BF16),
            pltpu.VMEM((8, TOK), F32),
            pltpu.VMEM((2, 8, TOK), F32),
            pltpu.VMEM((2, CHUNKS, BLOCKS, 16, QUARTER), BF16),
            pltpu.VMEM((2, CHUNKS, BLOCKS, 16, QUARTER), BF16),
            pltpu.VMEM((CHUNKS, BLOCKS, 16, 256), BF16),
            pltpu.VMEM((CHUNKS, BLOCKS, 16, 256), BF16),
            pltpu.VMEM((CHUNKS, BLOCKS, 1, 128), F32),
            pltpu.VMEM((CHUNKS, BLOCKS, 1, 128), F32),
            pltpu.VMEM((512, D), BF16),
            pltpu.VMEM((512, D), BF16),
            pltpu.VMEM((512, F), BF16),
            pltpu.VMEM((512, F), BF16),
            pltpu.VMEM((2, 256, 256), BF16),
            pltpu.VMEM((2, D, HALF), BF16),
            pltpu.VMEM((2, D, HALF), BF16),
            pltpu.VMEM((3, TOK, TOK), F32),
            pltpu.VMEM((3, TOK, D), F32),
            pltpu.VMEM((2, TOK, D), BF16),
            pltpu.VMEM((2, TOK, D), BF16),
            pltpu.VMEM((2, 8, TOK), F32),
            pltpu.VMEM((2, 8, TOK), F32),
            pltpu.SemaphoreType.REGULAR((6,)),
            dma((13,)), dma((2, 3)), dma((2, 3)), dma((4, 3)),
            dma((2, CHUNKS)), dma((2, CHUNKS)), dma((CHUNKS,)), dma((CHUNKS,)),
            dma((CHUNKS,)), dma((CHUNKS,)), dma((2, 2)), dma((2, 2)), dma, dma,
        ],
        compiler_params=pltpu.CompilerParams(
            collective_id=0, has_side_effects=True, vmem_limit_bytes=60 * 2**20
        ),
        cost_estimate=pl.CostEstimate(
            flops=2 * 512 * 1024 * 1024 * 6, bytes_accessed=7 * 2**20, transcendentals=512 * 1024
        ),
    )(
        tokens,
        cotangent,
        gate_values.T,
        expert_ids.T,
        keep_second.reshape(1, TOK),
        weight_in,
        weight_out,
    )
    grad_tokens, grad_gates, grad_in, grad_out = pl.pallas_call(
        finish,
        out_shape=tuple(jax.ShapeDtypeStruct(p.shape, p.dtype) for p in parts),
        in_specs=[vmem] * 4,
        out_specs=(hbm,) * 4,
        scratch_shapes=[dma((4,))],
    )(*(pltpu.with_memory_space_constraint(p, pltpu.VMEM) for p in parts))
    return grad_tokens, grad_gates.T, grad_in, grad_out


def solution(mesh):
    in_specs = (
        P(("rep", "expert"), None),
        P(("rep", "expert"), None),
        P(("rep", "expert"), None),
        P(("rep", "expert"), None),
        P(("rep", "expert")),
        P("expert", None, None),
        P("expert", None, None),
    )
    out_specs = (
        P(("rep", "expert"), None),
        P(("rep", "expert"), None),
        P("expert", None, "rep"),
        P("expert", None, "rep"),
    )
    return jax.shard_map(body, mesh=mesh, in_specs=in_specs, out_specs=out_specs, check_vma=False)
```

```python
import functools

import jax
import jax.numpy as jnp
from jax import lax
from jax.experimental import pallas as pl
from jax.experimental.pallas import tpu as pltpu
from jax.sharding import PartitionSpec as P

MESH = pl.DeviceIdType.MESH
F32, BF16, I32 = jnp.float32, jnp.bfloat16, jnp.int32
NZ, NY, NX = 8, 4, 4
PLANE = NY * NX
EXPERTS = NZ * PLANE
CAP = 4
TOK = 128
D = 1024
F = 1024
HALF = 512
QUARTER = 256
ORDER = (0, 4, 3, 5, 2, 6, 1, 7)
CHUNKS = 4
BLOCKS = EXPERTS // CHUNKS
ROWS = BLOCKS * 16
SLOTS = BLOCKS * CAP
RUNS = (
    ((0, 16, 0, 0), (16, 24, 1, 3), (24, 32, 2, -3)),
    ((0, 16, 1, 2), (16, 32, 2, -2)),
    ((0, 16, 1, 1), (16, 32, 2, -1)),
    ((0, 16, 1, 0), (16, 32, 2, 0)),
)
LEAVE = ((0, 1, 2, 3), (0, 1, 2, 3))
WORK = (3, 0, 1, 2)
STAY = ((0, 0), (3, 0), (3, 16))


def dot(a, b, contract):
    return lax.dot_general(a, b, (contract, ((), ())), preferred_element_type=F32)


def iota(shape, dim):
    return lax.broadcasted_iota(I32, shape, dim)


def gelu_parts(pre):
    const = 0.7978845608028654
    square = pre * pre
    inner = jnp.tanh(const * (pre + 0.044715 * square * pre))
    half = 0.5 * (1.0 + inner)
    slope = half + 0.5 * pre * (1.0 - inner * inner) * (
        const * (1.0 + 3.0 * 0.044715 * square)
    )
    return pre * half, slope


def kernel(
    tokens_hbm, cot_hbm, gates_hbm, ids_hbm, keep_hbm, win_hbm, wout_hbm,
    gtok_ref, ggate_ref, gwin_ref, gwout_ref,
    win, wout, win_t, wout_t, gates, ids_in, keep, xcat, xnear, meta, meta_near, send, recv, ret, back,
    score_ret, score_back, xrows, gorows, actrows, gprows, slopes, perm, wg_send, wg_recv,
    colcode, total, part_send, part_recv, score_send, score_recv,
    met_sem, load_sem, near_send, near_recv, stay_sem, send_sem, recv_sem, ret_sem, back_sem,
    sret_sem, sback_sem, part_ssem, part_rsem, wgs_sem, wgr_sem,
):
    me = lax.axis_index("expert")
    rep = lax.axis_index("rep")
    my_z, my_y, my_x = me // PLANE, (me // NX) % NY, me % NX

    def device(dz, dy, dx):
        return (
            rep,
            ((my_z + dz + NZ) % NZ) * PLANE
            + ((my_y + dy + NY) % NY) * NX
            + (my_x + dx + NX) % NX,
        )

    def near(side):
        return device(1 - 2 * side, 0, 0)

    loads = [
        pltpu.make_async_copy(ids_hbm, ids_in, load_sem.at[0]),
        pltpu.make_async_copy(gates_hbm, gates, load_sem.at[1]),
        pltpu.make_async_copy(keep_hbm, keep, load_sem.at[2]),
        pltpu.make_async_copy(win_hbm.at[0], win, load_sem.at[3]),
        pltpu.make_async_copy(wout_hbm.at[0], wout, load_sem.at[4]),
    ]
    row_loads = [
        [
            pltpu.make_async_copy(
                held.at[:, q * QUARTER:(q + 1) * QUARTER],
                xcat.at[kind, q * TOK:(q + 1) * TOK],
                load_sem.at[5 + 4 * kind + q],
            )
            for q in range(4)
        ]
        for kind, held in enumerate((tokens_hbm, cot_hbm))
    ]
    for load in row_loads[0] + loads[:3] + row_loads[1]:
        load.start()

    bar = pltpu.get_barrier_semaphore()

    beside = [[device(*(step * (axis == a) for a in range(3))) for step in (1, -1)] for axis in range(3)]
    for to in [to for pair in beside for to in pair] + [(1 - rep, me)]:
        pl.semaphore_signal(bar, inc=1, device_id=to, device_id_type=MESH)
    for load in loads[3:]:
        load.start()

    def know(axis, at):
        for to in beside[axis]:
            pl.semaphore_signal(met_sem.at[at], inc=1, device_id=to, device_id_type=MESH)
        pl.semaphore_wait(met_sem.at[at], 2)

    def hand_over(side):
        to = near(side)
        return [
            pltpu.make_async_remote_copy(
                meta, meta_near.at[side], near_send.at[side, 2], near_recv.at[side, 2],
                device_id=to, device_id_type=MESH,
            ) if kind == 2 else pltpu.make_async_remote_copy(
                xcat.at[kind], xnear.at[side, kind],
                near_send.at[side, kind], near_recv.at[side, kind],
                device_id=to, device_id_type=MESH,
            )
            for kind in range(3)
        ]

    handed = [hand_over(0), hand_over(1)]
    for load in row_loads[0]:
        load.wait()
    pl.semaphore_wait(bar, 7)
    for side in range(2):
        handed[side][0].start()

    for load in loads[:3]:
        load.wait()
    ids = ids_in[...]
    dz = (ids // PLANE - my_z + NZ) % NZ
    dy = ((ids // NX) % NY - my_y + NY) % NY
    dx = (ids % NX - my_x + NX) % NX
    pz = jnp.zeros_like(dz)
    for at, off in enumerate(ORDER):
        pz = jnp.where(dz == off, at, pz)
    place = pz * PLANE + dy * NX + dx
    first, second = place[0:1], place[1:2]
    hot0 = jnp.where(iota((EXPERTS, TOK), 0) == first, 1.0, 0.0)
    hot1 = jnp.where(iota((EXPERTS, TOK), 0) == second, 1.0, 0.0)
    upper = jnp.where(iota((TOK, TOK), 0) < iota((TOK, TOK), 1), 1.0, 0.0).astype(BF16)
    plain = ((1,), (0,))
    before0 = dot(hot0.astype(BF16), upper, plain)
    before1 = dot(hot1.astype(BF16), upper, plain) + jnp.sum(hot0, axis=1, keepdims=True)
    pos0 = jnp.sum(hot0 * before0, axis=0, keepdims=True)
    pos1 = jnp.sum(hot1 * before1, axis=0, keepdims=True)
    gate_low = gates[...].astype(BF16).astype(F32)
    meta[...] = jnp.concatenate(
        [
            first.astype(F32) * 16 + pos0,
            second.astype(F32) * 16 + pos1,
            gate_low[0:1],
            gate_low[1:2] * keep[...].astype(F32),
            jnp.zeros((4, TOK), F32),
        ],
        axis=0,
    )

    for side in range(2):
        handed[side][2].start()
    for load in row_loads[1]:
        load.wait()
    for side in range(2):
        handed[side][1].start()

    def quads(source):
        rows = meta[...] if source == 0 else meta_near[source - 1]
        code0, code1 = rows[0:1].astype(I32), rows[1:2].astype(I32)
        return (
            jnp.concatenate([code0 + 4 * q for q in range(4)], axis=1),
            jnp.concatenate([code1 + 4 * q for q in range(4)], axis=1),
            jnp.concatenate([rows[2:3]] * 4, axis=1),
            jnp.concatenate([rows[3:4]] * 4, axis=1),
        )

    def gather(kind, c, run, quad):
        lo, hi, source, _ = run
        row = iota(((hi - lo) * 16, 512), 0) + (c * BLOCKS + lo) * 16
        one, two = (1.0, 1.0) if kind == 0 else quad[2:]
        pick = jnp.where(row == quad[0], one, jnp.where(row == quad[1], two, 0.0))
        held = xcat[kind] if source == 0 else xnear[source - 1, kind]
        block = dot(pick.astype(BF16), held, plain).astype(BF16)
        send[kind, c, lo:hi] = block.reshape(hi - lo, 16, QUARTER)

    along_x = {
        sign: [lax.rem(my_x + (sign * dx) % NX, NX) for dx in range(NX)] for sign in (1, -1)
    }

    def each(c, run, sign, step):
        lo, hi, _, off = run
        plane = lax.rem(my_z + (sign * off) % NZ, NZ) * PLANE
        rows = lo // NX

        def four(row, skip):
            dy = lax.rem(row, NY)
            line = plane + lax.rem(my_y + (dy if sign == 1 else NY - dy), NY) * NX
            for dx in range(skip, NX):
                step(row * NX + dx, (rep, line + along_x[sign][dx]))

        if (c, lo) in STAY:
            four(rows, 1)
            rows += 1

        def turn(row, carry):
            four(row, 0)
            return carry

        lax.fori_loop(rows, hi // NX, turn, 0)

    def dispatch(kind, c, run):
        def go(b, to):
            pltpu.make_async_remote_copy(
                send.at[kind, c, b], recv.at[kind, c, b],
                send_sem.at[kind, c], recv_sem.at[kind, c],
                device_id=to, device_id_type=MESH,
            ).start()

        each(c, run, 1, go)

    def stay(sources, results, kind, c):
        return [
            pltpu.make_async_copy(sources.at[c, b], results.at[c, b], stay_sem.at[kind, i])
            for i, (at, b) in enumerate(STAY)
            if at == c
        ]

    def await_all(buffer, c, sem):
        count = BLOCKS - sum(at == c for at, _ in STAY)
        part = buffer.at[c, pl.ds(0, count)]
        pltpu.make_async_copy(part, part, sem.at[c]).wait()

    def stay_rows(kind, c):
        return stay(send.at[kind], recv.at[kind], kind, c)

    know(2, 0)
    know(1, 1)
    know(1, 2)
    own = quads(0)
    for kind in range(2):
        gather(kind, 0, RUNS[0][0], own)
        dispatch(kind, 0, RUNS[0][0])
        for copy in stay_rows(kind, 0):
            copy.start()

    def column_codes(source):
        rows = meta[...] if source == 0 else meta_near[source - 1]
        tall = jnp.concatenate([rows, jnp.zeros((TOK - 8, TOK), F32)], axis=0)
        colcode[source] = jnp.transpose(tall)

    column_codes(0)
    out_row = iota((256, 256), 0)
    in_row = ((out_row // 4) % 16) * 16 + (out_row // 64) * 4 + out_row % 4
    perm[0] = jnp.where(in_row == iota((256, 256), 1), 1.0, 0.0).astype(BF16)
    out_col = iota((256, 256), 1)
    in_col = ((out_col // 4) % 16) * 16 + (out_col // 64) * 4 + out_col % 4
    perm[1] = jnp.where(in_col == iota((256, 256), 0), 1.0, 0.0).astype(BF16)

    know(0, 3)
    know(0, 4)
    know(0, 5)
    for load in loads[3:]:
        load.wait()
    for r in range(0, D, 256):
        win_t[:, r:r + 256] = jnp.transpose(win[r:r + 256, :])
        wout_t[:, r:r + 256] = jnp.transpose(wout[r:r + 256, :])
    for side in range(2):
        handed[side][2].wait_recv()
    column_codes(1)
    column_codes(2)
    quad = [own, quads(1), quads(2)]
    for kind, order in enumerate(LEAVE):
        for side in range(2):
            handed[side][kind].wait_recv()
        for c in order:
            for run in RUNS[c]:
                if run[2] > 0:
                    gather(kind, c, run, quad[run[2]])
                    dispatch(kind, c, run)
            if c > 0:
                for copy in stay_rows(kind, c):
                    copy.start()

    def settle(kind, c, plain_rows):
        await_all(recv.at[kind], c, recv_sem.at[kind])
        for copy in stay_rows(kind, c):
            copy.wait()
        for g in range(2):
            packed = recv[kind, c, g * 16:(g + 1) * 16].reshape(256, QUARTER)
            sorted_rows = dot(perm[0], packed, plain).astype(BF16)
            at = slice(c * SLOTS + g * 64, c * SLOTS + (g + 1) * 64)
            for q in range(4):
                plain_rows[at, q * QUARTER:(q + 1) * QUARTER] = sorted_rows[q * 64:(q + 1) * 64]

    for c in WORK:
        settle(0, c, xrows)
        rows = slice(c * SLOTS, (c + 1) * SLOTS)
        act, slope = gelu_parts(dot(xrows[rows], win[...], plain))
        actrows[rows] = act.astype(BF16)
        slopes[rows] = slope

    for c in WORK:
        settle(1, c, gorows)
        rows = slice(c * SLOTS, (c + 1) * SLOTS)
        grad_act = dot(gorows[rows], wout_t[...], plain)
        act = actrows[rows]
        grad_pre = (grad_act * slopes[rows]).astype(BF16)
        gprows[rows] = grad_pre
        score = jnp.sum(act.astype(F32) * grad_act, axis=1, keepdims=True)
        spread = jnp.where(iota((SLOTS, 128), 0) % CAP == iota((SLOTS, 128), 1), score, 0.0)
        high = spread.astype(BF16)
        low = (spread - high.astype(F32)).astype(BF16)
        group = jnp.where(
            iota((BLOCKS, SLOTS), 1) // CAP == iota((BLOCKS, SLOTS), 0), 1.0, 0.0
        ).astype(BF16)
        score_ret[c] = (dot(group, high, plain) + dot(group, low, plain)).reshape(BLOCKS, 1, 128)
        grad_rows = dot(grad_pre, win_t[...], plain).astype(BF16)
        for g in range(2):
            piece = grad_rows[g * 64:(g + 1) * 64]
            stack = jnp.concatenate([piece[:, q * 256:(q + 1) * 256] for q in range(4)], axis=0)
            mixed = dot(perm[1], stack, plain).astype(BF16)
            ret[c, g * 16:(g + 1) * 16] = mixed.reshape(16, 16, 256)

        for run in RUNS[c]:
            def give(b, to, c=c):
                pltpu.make_async_remote_copy(
                    ret.at[c, b], back.at[c, b], ret_sem.at[c], back_sem.at[c],
                    device_id=to, device_id_type=MESH,
                ).start()
                pltpu.make_async_remote_copy(
                    score_ret.at[c, b], score_back.at[c, b], sret_sem.at[c], sback_sem.at[c],
                    device_id=to, device_id_type=MESH,
                ).start()

            each(c, run, -1, give)
        for copy in stay(ret, back, 2, c) + stay(score_ret, score_back, 3, c):
            copy.start()

    theirs = pl.multiple_of((1 - rep) * HALF, HALF)
    mine = pl.multiple_of(rep * HALF, HALF)
    down = ((0,), (0,))
    wg_send[0] = dot(xrows[...], gprows[:, pl.ds(theirs, HALF)], down).astype(BF16)
    wg_send[1] = dot(actrows[...], gorows[:, pl.ds(theirs, HALF)], down).astype(BF16)
    swap = pltpu.make_async_remote_copy(
        wg_send, wg_recv, wgs_sem, wgr_sem, device_id=(1 - rep, me), device_id_type=MESH
    )
    swap.start()

    started = set()
    for c in WORK:
        await_all(back, c, back_sem)
        for copy in stay(ret, back, 2, c):
            copy.wait()
        for lo, hi, source, _ in RUNS[c]:
            size = (hi - lo) * 16
            lane = iota((TOK, size), 1) + (c * BLOCKS + lo) * 16
            landed = back[c, lo:hi].reshape(size, 256)
            col0 = colcode[source, :, 0:1].astype(I32)
            col1 = colcode[source, :, 1:2].astype(I32)
            for q in range(4):
                pick = jnp.where(
                    lane == col0 + 4 * q, 1.0, jnp.where(lane == col1 + 4 * q, 1.0, 0.0)
                )
                piece = dot(pick.astype(BF16), landed, plain)
                where = slice(q * 256, (q + 1) * 256)
                if source in started:
                    piece = piece + total[source, :, where]
                if c == WORK[-1] and source > 0:
                    part_send[source - 1, :, where] = piece.astype(BF16)
                else:
                    total[source, :, where] = piece
            started.add(source)
            if c == WORK[-1] and source > 0:
                pltpu.make_async_remote_copy(
                    part_send.at[source - 1], part_recv.at[source - 1],
                    part_ssem.at[source - 1, 0], part_rsem.at[source - 1, 0],
                    device_id=near(2 - source), device_id_type=MESH,
                ).start()

    for c in range(CHUNKS):
        await_all(score_back, c, sback_sem)
        for copy in stay(score_ret, score_back, 3, c):
            copy.wait()
    scores = score_back[...].reshape(EXPERTS, 128)
    spot = iota((EXPERTS, TOK), 0)
    low_half = spot % BLOCKS < 16

    def score_rows(source):
        rows = meta[...] if source == 0 else meta_near[source - 1]
        if source == 0:
            here = spot < 16
        elif source == 1:
            here = ((spot >= BLOCKS) & low_half) | ((spot >= 16) & (spot < 24))
        else:
            here = ((spot >= BLOCKS) & jnp.logical_not(low_half)) | ((spot >= 24) & (spot < BLOCKS))
        found = []
        for k in range(2):
            code = rows[k:k + 1].astype(I32)
            hot = jnp.where((spot == code // 16) & here, 1.0, 0.0)
            got = jnp.zeros((1, TOK), F32)
            for s in range(CAP):
                hit = jnp.sum(hot * scores[:, s:s + 1], axis=0, keepdims=True)
                got = got + jnp.where(code % 16 == s, hit, 0.0)
            found.append(got)
        return jnp.concatenate(found + [jnp.zeros((6, TOK), F32)], axis=0)

    for source in (1, 2):
        score_send[source - 1] = score_rows(source)
        pltpu.make_async_remote_copy(
            score_send.at[source - 1], score_recv.at[source - 1],
            part_ssem.at[source - 1, 1], part_rsem.at[source - 1, 1],
            device_id=near(2 - source), device_id_type=MESH,
        ).start()
    own_scores = score_rows(0)

    own_in = dot(xrows[...], gprows[:, pl.ds(mine, HALF)], down)
    own_out = dot(actrows[...], gorows[:, pl.ds(mine, HALF)], down)
    swap.wait()
    gwin_ref[0] = (own_in + wg_recv[0].astype(F32)).astype(BF16)
    gwout_ref[0] = (own_out + wg_recv[1].astype(F32)).astype(BF16)

    for side in range(2):
        for kind, (sent, landed) in enumerate(((part_send, part_recv), (score_send, score_recv))):
            pltpu.make_async_remote_copy(
                sent.at[side], landed.at[side], part_ssem.at[side, kind], part_rsem.at[side, kind],
                device_id=near(1 - side), device_id_type=MESH,
            ).wait()
    gtok_ref[...] = (
        total[0] + part_recv[0].astype(F32) + part_recv[1].astype(F32)
    ).astype(BF16)
    all_scores = own_scores + score_recv[0] + score_recv[1]
    ggate_ref[...] = all_scores[0:2] / gate_low

    for side in range(2):
        for part in range(3):
            handed[side][part].wait_send()
    for c in range(CHUNKS):
        for kind in range(2):
            await_all(send.at[kind], c, send_sem.at[kind])
        await_all(ret, c, ret_sem)
        await_all(score_ret, c, sret_sem)


def finish(*refs):
    sources, results, sems = refs[:4], refs[4:8], refs[8]
    for i in range(4):
        pltpu.make_async_copy(sources[i], results[i], sems.at[i]).start()
    for i in range(4):
        pltpu.make_async_copy(sources[i], results[i], sems.at[i]).wait()


def body(tokens, cotangent, gate_values, expert_ids, keep_second, weight_in, weight_out):
    vmem = pl.BlockSpec(memory_space=pltpu.VMEM)
    hbm = pl.BlockSpec(memory_space=pl.ANY)
    dma = pltpu.SemaphoreType.DMA
    parts = pl.pallas_call(
        kernel,
        out_shape=(
            pltpu.VMEM((TOK, D), BF16),
            pltpu.VMEM((2, TOK), F32),
            pltpu.VMEM((1, D, HALF), BF16),
            pltpu.VMEM((1, F, HALF), BF16),
        ),
        in_specs=[hbm] * 7,
        out_specs=(vmem,) * 4,
        scratch_shapes=[
            pltpu.VMEM((D, F), BF16),
            pltpu.VMEM((F, D), BF16),
            pltpu.VMEM((F, D), BF16),
            pltpu.VMEM((D, F), BF16),
            pltpu.VMEM((2, TOK), F32),
            pltpu.VMEM((2, TOK), I32),
            pltpu.VMEM((1, TOK), I32),
            pltpu.VMEM((2, 512, QUARTER), BF16),
            pltpu.VMEM((2, 2, 512, QUARTER), BF16),
            pltpu.VMEM((8, TOK), F32),
            pltpu.VMEM((2, 8, TOK), F32),
            pltpu.VMEM((2, CHUNKS, BLOCKS, 16, QUARTER), BF16),
            pltpu.VMEM((2, CHUNKS, BLOCKS, 16, QUARTER), BF16),
            pltpu.VMEM((CHUNKS, BLOCKS, 16, 256), BF16),
            pltpu.VMEM((CHUNKS, BLOCKS, 16, 256), BF16),
            pltpu.VMEM((CHUNKS, BLOCKS, 1, 128), F32),
            pltpu.VMEM((CHUNKS, BLOCKS, 1, 128), F32),
            pltpu.VMEM((512, D), BF16),
            pltpu.VMEM((512, D), BF16),
            pltpu.VMEM((512, F), BF16),
            pltpu.VMEM((512, F), BF16),
            pltpu.VMEM((512, F), F32),
            pltpu.VMEM((2, 256, 256), BF16),
            pltpu.VMEM((2, D, HALF), BF16),
            pltpu.VMEM((2, D, HALF), BF16),
            pltpu.VMEM((3, TOK, TOK), F32),
            pltpu.VMEM((3, TOK, D), F32),
            pltpu.VMEM((2, TOK, D), BF16),
            pltpu.VMEM((2, TOK, D), BF16),
            pltpu.VMEM((2, 8, TOK), F32),
            pltpu.VMEM((2, 8, TOK), F32),
            pltpu.SemaphoreType.REGULAR((6,)),
            dma((13,)), dma((2, 3)), dma((2, 3)), dma((4, 3)),
            dma((2, CHUNKS)), dma((2, CHUNKS)), dma((CHUNKS,)), dma((CHUNKS,)),
            dma((CHUNKS,)), dma((CHUNKS,)), dma((2, 2)), dma((2, 2)), dma, dma,
        ],
        compiler_params=pltpu.CompilerParams(
            collective_id=0, has_side_effects=True, vmem_limit_bytes=60 * 2**20
        ),
        cost_estimate=pl.CostEstimate(
            flops=2 * 512 * 1024 * 1024 * 6, bytes_accessed=7 * 2**20, transcendentals=512 * 1024
        ),
    )(
        tokens,
        cotangent,
        gate_values.T,
        expert_ids.T,
        keep_second.reshape(1, TOK),
        weight_in,
        weight_out,
    )
    grad_tokens, grad_gates, grad_in, grad_out = pl.pallas_call(
        finish,
        out_shape=tuple(jax.ShapeDtypeStruct(p.shape, p.dtype) for p in parts),
        in_specs=[vmem] * 4,
        out_specs=(hbm,) * 4,
        scratch_shapes=[dma((4,))],
    )(*(pltpu.with_memory_space_constraint(p, pltpu.VMEM) for p in parts))
    return grad_tokens, grad_gates.T, grad_in, grad_out


def solution(mesh):
    in_specs = (
        P(("rep", "expert"), None),
        P(("rep", "expert"), None),
        P(("rep", "expert"), None),
        P(("rep", "expert"), None),
        P(("rep", "expert")),
        P("expert", None, None),
        P("expert", None, None),
    )
    out_specs = (
        P(("rep", "expert"), None),
        P(("rep", "expert"), None),
        P("expert", None, "rep"),
        P("expert", None, "rep"),
    )
    return jax.shard_map(body, mesh=mesh, in_specs=in_specs, out_specs=out_specs, check_vma=False)
```

```python
import functools

import jax
import jax.numpy as jnp
from jax import lax
from jax.experimental import pallas as pl
from jax.experimental.pallas import tpu as pltpu
from jax.sharding import PartitionSpec as P

MESH = pl.DeviceIdType.MESH
F32, BF16, I32 = jnp.float32, jnp.bfloat16, jnp.int32
NZ, NY, NX = 8, 4, 4
PLANE = NY * NX
EXPERTS = NZ * PLANE
CAP = 4
TOK = 128
D = 1024
F = 1024
HALF = 512
QUARTER = 256
ORDER = (0, 4, 3, 5, 2, 6, 1, 7)
CHUNKS = 4
BLOCKS = EXPERTS // CHUNKS
ROWS = BLOCKS * 16
SLOTS = BLOCKS * CAP
RUNS = (
    ((0, 16, 0, 0), (16, 24, 1, 3), (24, 32, 2, -3)),
    ((0, 16, 1, 2), (16, 32, 2, -2)),
    ((0, 16, 1, 1), (16, 32, 2, -1)),
    ((0, 16, 1, 0), (16, 32, 2, 0)),
)
LEAVE = ((0, 1, 2, 3), (0, 1, 2, 3))
WORK = (3, 0, 1, 2)
STAY = ((0, 0), (3, 0), (3, 16))


def dot(a, b, contract):
    return lax.dot_general(a, b, (contract, ((), ())), preferred_element_type=F32)


def iota(shape, dim):
    return lax.broadcasted_iota(I32, shape, dim)


def gelu_parts(pre):
    const = 0.7978845608028654
    square = pre * pre
    inner = jnp.tanh(const * (pre + 0.044715 * square * pre))
    half = 0.5 * (1.0 + inner)
    slope = half + 0.5 * pre * (1.0 - inner * inner) * (
        const * (1.0 + 3.0 * 0.044715 * square)
    )
    return pre * half, slope


def kernel(
    tokens_hbm, cot_hbm, gates_hbm, ids_hbm, keep_hbm, win_hbm, wout_hbm,
    gtok_ref, ggate_ref, gwin_ref, gwout_ref,
    win, wout, win_t, wout_t, gates, ids_in, keep, xcat, xnear, meta, meta_near, send, recv, ret, back,
    score_ret, score_back, xrows, gorows, actrows, gprows, slopes, perm, wg_send, wg_recv,
    colcode, total, part_send, part_recv, score_send, score_recv,
    met_sem, load_sem, near_send, near_recv, stay_sem, send_sem, recv_sem, ret_sem, back_sem,
    sret_sem, sback_sem, part_ssem, part_rsem, wgs_sem, wgr_sem,
):
    me = lax.axis_index("expert")
    rep = lax.axis_index("rep")
    my_z, my_y, my_x = me // PLANE, (me // NX) % NY, me % NX

    def device(dz, dy, dx):
        return (
            rep,
            ((my_z + dz + NZ) % NZ) * PLANE
            + ((my_y + dy + NY) % NY) * NX
            + (my_x + dx + NX) % NX,
        )

    def near(side):
        return device(1 - 2 * side, 0, 0)

    loads = [
        pltpu.make_async_copy(ids_hbm, ids_in, load_sem.at[0]),
        pltpu.make_async_copy(gates_hbm, gates, load_sem.at[1]),
        pltpu.make_async_copy(keep_hbm, keep, load_sem.at[2]),
        pltpu.make_async_copy(win_hbm.at[0], win, load_sem.at[3]),
        pltpu.make_async_copy(wout_hbm.at[0], wout, load_sem.at[4]),
    ]
    row_loads = [
        [
            pltpu.make_async_copy(
                held.at[:, q * QUARTER:(q + 1) * QUARTER],
                xcat.at[kind, q * TOK:(q + 1) * TOK],
                load_sem.at[5 + 4 * kind + q],
            )
            for q in range(4)
        ]
        for kind, held in enumerate((tokens_hbm, cot_hbm))
    ]
    for load in row_loads[0] + loads[:3] + row_loads[1]:
        load.start()

    bar = pltpu.get_barrier_semaphore()

    beside = [[device(*(step * (axis == a) for a in range(3))) for step in (1, -1)] for axis in range(3)]
    for to in [to for pair in beside for to in pair] + [(1 - rep, me)]:
        pl.semaphore_signal(bar, inc=1, device_id=to, device_id_type=MESH)
    for load in loads[3:]:
        load.start()

    def know(axis, at):
        for to in beside[axis]:
            pl.semaphore_signal(met_sem.at[at], inc=1, device_id=to, device_id_type=MESH)
        pl.semaphore_wait(met_sem.at[at], 2)

    def hand_over(side):
        to = near(side)
        return [
            pltpu.make_async_remote_copy(
                meta, meta_near.at[side], near_send.at[side, 2], near_recv.at[side, 2],
                device_id=to, device_id_type=MESH,
            ) if kind == 2 else pltpu.make_async_remote_copy(
                xcat.at[kind], xnear.at[side, kind],
                near_send.at[side, kind], near_recv.at[side, kind],
                device_id=to, device_id_type=MESH,
            )
            for kind in range(3)
        ]

    handed = [hand_over(0), hand_over(1)]
    for load in row_loads[0]:
        load.wait()
    pl.semaphore_wait(bar, 7)
    for side in range(2):
        handed[side][0].start()

    for load in loads[:3]:
        load.wait()
    ids = ids_in[...]
    dz = (ids // PLANE - my_z + NZ) % NZ
    dy = ((ids // NX) % NY - my_y + NY) % NY
    dx = (ids % NX - my_x + NX) % NX
    pz = jnp.zeros_like(dz)
    for at, off in enumerate(ORDER):
        pz = jnp.where(dz == off, at, pz)
    place = pz * PLANE + dy * NX + dx
    first, second = place[0:1], place[1:2]
    hot0 = jnp.where(iota((EXPERTS, TOK), 0) == first, 1.0, 0.0)
    hot1 = jnp.where(iota((EXPERTS, TOK), 0) == second, 1.0, 0.0)
    upper = jnp.where(iota((TOK, TOK), 0) < iota((TOK, TOK), 1), 1.0, 0.0).astype(BF16)
    plain = ((1,), (0,))
    before0 = dot(hot0.astype(BF16), upper, plain)
    before1 = dot(hot1.astype(BF16), upper, plain) + jnp.sum(hot0, axis=1, keepdims=True)
    pos0 = jnp.sum(hot0 * before0, axis=0, keepdims=True)
    pos1 = jnp.sum(hot1 * before1, axis=0, keepdims=True)
    gate_low = gates[...].astype(BF16).astype(F32)
    meta[...] = jnp.concatenate(
        [
            first.astype(F32) * 16 + pos0,
            second.astype(F32) * 16 + pos1,
            gate_low[0:1],
            gate_low[1:2] * keep[...].astype(F32),
            jnp.zeros((4, TOK), F32),
        ],
        axis=0,
    )

    for side in range(2):
        handed[side][2].start()
    for load in row_loads[1]:
        load.wait()
    for side in range(2):
        handed[side][1].start()

    def quads(source):
        rows = meta[...] if source == 0 else meta_near[source - 1]
        code0, code1 = rows[0:1].astype(I32), rows[1:2].astype(I32)
        return (
            jnp.concatenate([code0 + 4 * q for q in range(4)], axis=1),
            jnp.concatenate([code1 + 4 * q for q in range(4)], axis=1),
            jnp.concatenate([rows[2:3]] * 4, axis=1),
            jnp.concatenate([rows[3:4]] * 4, axis=1),
        )

    def gather(kind, c, run, quad):
        lo, hi, source, _ = run
        row = iota(((hi - lo) * 16, 512), 0) + (c * BLOCKS + lo) * 16
        one, two = (1.0, 1.0) if kind == 0 else quad[2:]
        pick = jnp.where(row == quad[0], one, jnp.where(row == quad[1], two, 0.0))
        held = xcat[kind] if source == 0 else xnear[source - 1, kind]
        block = dot(pick.astype(BF16), held, plain).astype(BF16)
        send[kind, c, lo:hi] = block.reshape(hi - lo, 16, QUARTER)

    along_x = {
        sign: [lax.rem(my_x + (sign * dx) % NX, NX) for dx in range(NX)] for sign in (1, -1)
    }

    def each(c, run, sign, step):
        lo, hi, _, off = run
        plane = lax.rem(my_z + (sign * off) % NZ, NZ) * PLANE
        rows = lo // NX

        def four(row, skip):
            dy = lax.rem(row, NY)
            line = plane + lax.rem(my_y + (dy if sign == 1 else NY - dy), NY) * NX
            for dx in range(skip, NX):
                step(row * NX + dx, (rep, line + along_x[sign][dx]))

        if (c, lo) in STAY:
            four(rows, 1)
            rows += 1

        def turn(row, carry):
            four(row, 0)
            return carry

        lax.fori_loop(rows, hi // NX, turn, 0)

    def dispatch(kind, c, run):
        def go(b, to):
            pltpu.make_async_remote_copy(
                send.at[kind, c, b], recv.at[kind, c, b],
                send_sem.at[kind, c], recv_sem.at[kind, c],
                device_id=to, device_id_type=MESH,
            ).start()

        each(c, run, 1, go)

    def stay(sources, results, kind, c):
        return [
            pltpu.make_async_copy(sources.at[c, b], results.at[c, b], stay_sem.at[kind, i])
            for i, (at, b) in enumerate(STAY)
            if at == c
        ]

    def await_all(buffer, c, sem):
        count = BLOCKS - sum(at == c for at, _ in STAY)
        part = buffer.at[c, pl.ds(0, count)]
        pltpu.make_async_copy(part, part, sem.at[c]).wait()

    def stay_rows(kind, c):
        return stay(send.at[kind], recv.at[kind], kind, c)

    know(2, 0)
    know(1, 1)
    know(1, 2)
    own = quads(0)
    for kind in range(2):
        gather(kind, 0, RUNS[0][0], own)
        dispatch(kind, 0, RUNS[0][0])
        for copy in stay_rows(kind, 0):
            copy.start()

    def column_codes(source):
        rows = meta[...] if source == 0 else meta_near[source - 1]
        tall = jnp.concatenate([rows, jnp.zeros((TOK - 8, TOK), F32)], axis=0)
        colcode[source] = jnp.transpose(tall)

    column_codes(0)
    out_row = iota((256, 256), 0)
    in_row = ((out_row // 4) % 16) * 16 + (out_row // 64) * 4 + out_row % 4
    perm[0] = jnp.where(in_row == iota((256, 256), 1), 1.0, 0.0).astype(BF16)
    out_col = iota((256, 256), 1)
    in_col = ((out_col // 4) % 16) * 16 + (out_col // 64) * 4 + out_col % 4
    perm[1] = jnp.where(in_col == iota((256, 256), 0), 1.0, 0.0).astype(BF16)

    know(0, 3)
    know(0, 4)
    know(0, 5)
    for load in loads[3:]:
        load.wait()
    for r in range(0, D, 256):
        win_t[:, r:r + 256] = jnp.transpose(win[r:r + 256, :])
        wout_t[:, r:r + 256] = jnp.transpose(wout[r:r + 256, :])
    for side in range(2):
        handed[side][2].wait_recv()
    column_codes(1)
    column_codes(2)
    quad = [own, quads(1), quads(2)]
    for kind, order in enumerate(LEAVE):
        for side in range(2):
            handed[side][kind].wait_recv()
        for c in order:
            for run in RUNS[c]:
                if run[2] > 0:
                    gather(kind, c, run, quad[run[2]])
                    dispatch(kind, c, run)
            if c > 0:
                for copy in stay_rows(kind, c):
                    copy.start()

    def settle(kind, c, plain_rows):
        await_all(recv.at[kind], c, recv_sem.at[kind])
        for copy in stay_rows(kind, c):
            copy.wait()
        for g in range(2):
            packed = recv[kind, c, g * 16:(g + 1) * 16].reshape(256, QUARTER)
            sorted_rows = dot(perm[0], packed, plain).astype(BF16)
            at = slice(c * SLOTS + g * 64, c * SLOTS + (g + 1) * 64)
            for q in range(4):
                plain_rows[at, q * QUARTER:(q + 1) * QUARTER] = sorted_rows[q * 64:(q + 1) * 64]

    for c in WORK:
        settle(0, c, xrows)
        rows = slice(c * SLOTS, (c + 1) * SLOTS)
        act, slope = gelu_parts(dot(xrows[rows], win[...], plain))
        actrows[rows] = act.astype(BF16)
        slopes[rows] = slope

    for c in WORK:
        settle(1, c, gorows)
        rows = slice(c * SLOTS, (c + 1) * SLOTS)
        grad_act = dot(gorows[rows], wout_t[...], plain)
        act = actrows[rows]
        grad_pre = (grad_act * slopes[rows]).astype(BF16)
        gprows[rows] = grad_pre
        score = jnp.sum(act.astype(F32) * grad_act, axis=1, keepdims=True)
        spread = jnp.where(iota((SLOTS, 128), 0) % CAP == iota((SLOTS, 128), 1), score, 0.0)
        high = spread.astype(BF16)
        low = (spread - high.astype(F32)).astype(BF16)
        group = jnp.where(
            iota((BLOCKS, SLOTS), 1) // CAP == iota((BLOCKS, SLOTS), 0), 1.0, 0.0
        ).astype(BF16)
        score_ret[c] = (dot(group, high, plain) + dot(group, low, plain)).reshape(BLOCKS, 1, 128)
        grad_rows = dot(grad_pre, win_t[...], plain).astype(BF16)
        for g in range(2):
            piece = grad_rows[g * 64:(g + 1) * 64]
            stack = jnp.concatenate([piece[:, q * 256:(q + 1) * 256] for q in range(4)], axis=0)
            mixed = dot(perm[1], stack, plain).astype(BF16)
            ret[c, g * 16:(g + 1) * 16] = mixed.reshape(16, 16, 256)

        for run in RUNS[c]:
            def give(b, to, c=c):
                pltpu.make_async_remote_copy(
                    ret.at[c, b], back.at[c, b], ret_sem.at[c], back_sem.at[c],
                    device_id=to, device_id_type=MESH,
                ).start()
                pltpu.make_async_remote_copy(
                    score_ret.at[c, b], score_back.at[c, b], sret_sem.at[c], sback_sem.at[c],
                    device_id=to, device_id_type=MESH,
                ).start()

            each(c, run, -1, give)
        for copy in stay(ret, back, 2, c) + stay(score_ret, score_back, 3, c):
            copy.start()

    theirs = pl.multiple_of((1 - rep) * HALF, HALF)
    mine = pl.multiple_of(rep * HALF, HALF)
    down = ((0,), (0,))
    wg_send[0] = dot(xrows[...], gprows[:, pl.ds(theirs, HALF)], down).astype(BF16)
    wg_send[1] = dot(actrows[...], gorows[:, pl.ds(theirs, HALF)], down).astype(BF16)
    swap = pltpu.make_async_remote_copy(
        wg_send, wg_recv, wgs_sem, wgr_sem, device_id=(1 - rep, me), device_id_type=MESH
    )
    swap.start()

    def hand_back(source, q):
        side, where = source - 1, slice(q * QUARTER, (q + 1) * QUARTER)
        return pltpu.make_async_remote_copy(
            part_send.at[side, :, where], part_recv.at[side, :, where],
            part_ssem.at[side, q], part_rsem.at[side, q],
            device_id=near(2 - source), device_id_type=MESH,
        )

    def picks_of(c, run):
        lo, hi, source, _ = run
        lane = iota((TOK, (hi - lo) * 16), 1) + (c * BLOCKS + lo) * 16
        col0 = colcode[source, :, 0:1].astype(I32)
        col1 = colcode[source, :, 1:2].astype(I32)
        return [
            jnp.where(
                lane == col0 + 4 * q, 1.0, jnp.where(lane == col1 + 4 * q, 1.0, 0.0)
            ).astype(BF16)
            for q in range(4)
        ]

    started = set()
    for c in WORK:
        last = c == WORK[-1]
        if last:
            own_in = dot(xrows[...], gprows[:, pl.ds(mine, HALF)], down)
            own_out = dot(actrows[...], gorows[:, pl.ds(mine, HALF)], down)
        picks = [picks_of(c, run) for run in RUNS[c]]
        await_all(back, c, back_sem)
        for copy in stay(ret, back, 2, c):
            copy.wait()
        for q in range(4):
            where = slice(q * QUARTER, (q + 1) * QUARTER)
            for pick, (lo, hi, source, _) in zip(picks, RUNS[c]):
                landed = back[c, lo:hi].reshape((hi - lo) * 16, QUARTER)
                piece = dot(pick[q], landed, plain)
                if source in started:
                    piece = piece + total[source, :, where]
                if last and source > 0:
                    part_send[source - 1, :, where] = piece.astype(BF16)
                    hand_back(source, q).start()
                else:
                    total[source, :, where] = piece
        started.update(run[2] for run in RUNS[c])

    for c in range(CHUNKS):
        await_all(score_back, c, sback_sem)
        for copy in stay(score_ret, score_back, 3, c):
            copy.wait()
    scores = score_back[...].reshape(EXPERTS, 128)
    spot = iota((EXPERTS, TOK), 0)
    low_half = spot % BLOCKS < 16

    def score_rows(source):
        rows = meta[...] if source == 0 else meta_near[source - 1]
        if source == 0:
            here = spot < 16
        elif source == 1:
            here = ((spot >= BLOCKS) & low_half) | ((spot >= 16) & (spot < 24))
        else:
            here = ((spot >= BLOCKS) & jnp.logical_not(low_half)) | ((spot >= 24) & (spot < BLOCKS))
        found = []
        for k in range(2):
            code = rows[k:k + 1].astype(I32)
            hot = jnp.where((spot == code // 16) & here, 1.0, 0.0)
            got = jnp.zeros((1, TOK), F32)
            for s in range(CAP):
                hit = jnp.sum(hot * scores[:, s:s + 1], axis=0, keepdims=True)
                got = got + jnp.where(code % 16 == s, hit, 0.0)
            found.append(got)
        return jnp.concatenate(found + [jnp.zeros((6, TOK), F32)], axis=0)

    for source in (1, 2):
        score_send[source - 1] = score_rows(source)
        pltpu.make_async_remote_copy(
            score_send.at[source - 1], score_recv.at[source - 1],
            part_ssem.at[source - 1, 4], part_rsem.at[source - 1, 4],
            device_id=near(2 - source), device_id_type=MESH,
        ).start()
    own_scores = score_rows(0)

    swap.wait()
    gwin_ref[0] = (own_in + wg_recv[0].astype(F32)).astype(BF16)
    gwout_ref[0] = (own_out + wg_recv[1].astype(F32)).astype(BF16)

    for source in (1, 2):
        for q in range(4):
            hand_back(source, q).wait()
        pltpu.make_async_remote_copy(
            score_send.at[source - 1], score_recv.at[source - 1],
            part_ssem.at[source - 1, 4], part_rsem.at[source - 1, 4],
            device_id=near(2 - source), device_id_type=MESH,
        ).wait()
    gtok_ref[...] = (
        total[0] + part_recv[0].astype(F32) + part_recv[1].astype(F32)
    ).astype(BF16)
    all_scores = own_scores + score_recv[0] + score_recv[1]
    ggate_ref[...] = all_scores[0:2] / gate_low

    for side in range(2):
        for part in range(3):
            handed[side][part].wait_send()
    for c in range(CHUNKS):
        for kind in range(2):
            await_all(send.at[kind], c, send_sem.at[kind])
        await_all(ret, c, ret_sem)
        await_all(score_ret, c, sret_sem)


def finish(*refs):
    sources, results, sems = refs[:4], refs[4:8], refs[8]
    for i in range(4):
        pltpu.make_async_copy(sources[i], results[i], sems.at[i]).start()
    for i in range(4):
        pltpu.make_async_copy(sources[i], results[i], sems.at[i]).wait()


def body(tokens, cotangent, gate_values, expert_ids, keep_second, weight_in, weight_out):
    vmem = pl.BlockSpec(memory_space=pltpu.VMEM)
    hbm = pl.BlockSpec(memory_space=pl.ANY)
    dma = pltpu.SemaphoreType.DMA
    parts = pl.pallas_call(
        kernel,
        out_shape=(
            pltpu.VMEM((TOK, D), BF16),
            pltpu.VMEM((2, TOK), F32),
            pltpu.VMEM((1, D, HALF), BF16),
            pltpu.VMEM((1, F, HALF), BF16),
        ),
        in_specs=[hbm] * 7,
        out_specs=(vmem,) * 4,
        scratch_shapes=[
            pltpu.VMEM((D, F), BF16),
            pltpu.VMEM((F, D), BF16),
            pltpu.VMEM((F, D), BF16),
            pltpu.VMEM((D, F), BF16),
            pltpu.VMEM((2, TOK), F32),
            pltpu.VMEM((2, TOK), I32),
            pltpu.VMEM((1, TOK), I32),
            pltpu.VMEM((2, 512, QUARTER), BF16),
            pltpu.VMEM((2, 2, 512, QUARTER), BF16),
            pltpu.VMEM((8, TOK), F32),
            pltpu.VMEM((2, 8, TOK), F32),
            pltpu.VMEM((2, CHUNKS, BLOCKS, 16, QUARTER), BF16),
            pltpu.VMEM((2, CHUNKS, BLOCKS, 16, QUARTER), BF16),
            pltpu.VMEM((CHUNKS, BLOCKS, 16, 256), BF16),
            pltpu.VMEM((CHUNKS, BLOCKS, 16, 256), BF16),
            pltpu.VMEM((CHUNKS, BLOCKS, 1, 128), F32),
            pltpu.VMEM((CHUNKS, BLOCKS, 1, 128), F32),
            pltpu.VMEM((512, D), BF16),
            pltpu.VMEM((512, D), BF16),
            pltpu.VMEM((512, F), BF16),
            pltpu.VMEM((512, F), BF16),
            pltpu.VMEM((512, F), F32),
            pltpu.VMEM((2, 256, 256), BF16),
            pltpu.VMEM((2, D, HALF), BF16),
            pltpu.VMEM((2, D, HALF), BF16),
            pltpu.VMEM((3, TOK, TOK), F32),
            pltpu.VMEM((3, TOK, D), F32),
            pltpu.VMEM((2, TOK, D), BF16),
            pltpu.VMEM((2, TOK, D), BF16),
            pltpu.VMEM((2, 8, TOK), F32),
            pltpu.VMEM((2, 8, TOK), F32),
            pltpu.SemaphoreType.REGULAR((6,)),
            dma((13,)), dma((2, 3)), dma((2, 3)), dma((4, 3)),
            dma((2, CHUNKS)), dma((2, CHUNKS)), dma((CHUNKS,)), dma((CHUNKS,)),
            dma((CHUNKS,)), dma((CHUNKS,)), dma((2, 5)), dma((2, 5)), dma, dma,
        ],
        compiler_params=pltpu.CompilerParams(
            collective_id=0, has_side_effects=True, vmem_limit_bytes=60 * 2**20
        ),
        cost_estimate=pl.CostEstimate(
            flops=2 * 512 * 1024 * 1024 * 6, bytes_accessed=7 * 2**20, transcendentals=512 * 1024
        ),
    )(
        tokens,
        cotangent,
        gate_values.T,
        expert_ids.T,
        keep_second.reshape(1, TOK),
        weight_in,
        weight_out,
    )
    grad_tokens, grad_gates, grad_in, grad_out = pl.pallas_call(
        finish,
        out_shape=tuple(jax.ShapeDtypeStruct(p.shape, p.dtype) for p in parts),
        in_specs=[vmem] * 4,
        out_specs=(hbm,) * 4,
        scratch_shapes=[dma((4,))],
    )(*(pltpu.with_memory_space_constraint(p, pltpu.VMEM) for p in parts))
    return grad_tokens, grad_gates.T, grad_in, grad_out


def solution(mesh):
    in_specs = (
        P(("rep", "expert"), None),
        P(("rep", "expert"), None),
        P(("rep", "expert"), None),
        P(("rep", "expert"), None),
        P(("rep", "expert")),
        P("expert", None, None),
        P("expert", None, None),
    )
    out_specs = (
        P(("rep", "expert"), None),
        P(("rep", "expert"), None),
        P("expert", None, "rep"),
        P("expert", None, "rep"),
    )
    return jax.shard_map(body, mesh=mesh, in_specs=in_specs, out_specs=out_specs, check_vma=False)
```
